32 devices in a mesh: win: 16 (over z, y, x), state: 2 (over core).
Axes of the slice: x: 2, y: 2, z: 4, core: 2. Of those that a mesh axis runs over, the one named last changes fastest.
Arguments:
- anomalies: float32 [16, 512, 256], P('win', 'state'), may hold values from -12 to 12
- mean_state: float32 [16, 512], P('win', 'state'), may hold values from -6 to 6
- obs_rows: int32 [16, 256], P('win', 'state'), may hold values from 0 to 255
- obs_precision: float32 [16, 256], P('win', 'state'), may hold values from 0.03125 to 0.3125
Outputs:
- updated: float32 [16, 512, 256], P('win', 'state')
The draws below stay inside these ranges and needn't reach their ends.
Inputs may be any that keep to these rules, and one draw needn't show every extreme that they name: Observation j of window w reads state row (j // 128) * 256 + obs_rows[w, j], a row of the same block of 256 rows.
All inputs are finite; a program needn't handle non-finite values.
Results may differ from the reference program's by a relative error of at most 0.0003.
Values sent between devices are 32-bit elements; how exact they have to be, the bound alone decides.
A program may use at most 128 MiB of HBM per device.

```python
import math
import jax
import jax.numpy as jnp
from jax import lax

MEMBERS = 256
ROWS_DEV = 256
OBS_DEV = 128
OUTER = 1
NS_STEPS = 3
WINDOWS = 16
ROWS = 512
OBS = 256


def draw_anomalies(key, part):
    key_scale, key_noise = jax.random.split(key, 2)
    log_scale = jax.random.uniform(key_scale, (WINDOWS, ROWS, 1), jnp.float32, math.log(0.3), math.log(3.0))
    values = jax.random.normal(key_noise, (WINDOWS, ROWS, MEMBERS), jnp.float32) * jnp.exp(log_scale)
    return jnp.clip(values, -12.0, 12.0).astype(jnp.float32)


def with_ends(values, rng, low, high):
    spot = [jax.random.randint(jax.random.fold_in(rng, axis), (), 0, length) for axis, length in enumerate(values.shape)]
    main_axis = values.shape.index(max(values.shape))
    next_to = spot[:main_axis] + [(spot[main_axis] + 1) % values.shape[main_axis]] + spot[main_axis + 1:]
    return values.at[tuple(spot)].set(low).at[tuple(next_to)].set(high)


def shard_levels(key, extent, cuts, low, high):
    level, own = 1.0, jax.random.fold_in(key, 6)
    for dim, blocks in cuts:
        steps = jnp.exp(jax.random.uniform(jax.random.fold_in(own, dim), (blocks,), jnp.float32, low / len(cuts), high / len(cuts)))
        level = level * jnp.repeat(steps, extent[dim] // blocks).reshape([-1 if axis == dim else 1 for axis in range(len(extent))])
    return level


def bell_draw(own_key, dims, scale, limit, cuts=(), kind=jnp.bfloat16):
    drawn = jax.random.normal(own_key, dims, jnp.float32) * scale
    if len(cuts) > 0:
        drawn = shard_levels(own_key, dims, cuts, -0.22, 0.18) * drawn
    return jnp.clip(drawn, min=-limit, max=limit).astype(kind)


def setup_inputs(seed: int = 0) -> dict:
    splits = jax.random.split(jax.random.key(seed), 5)
    return {
        "anomalies": draw_anomalies(jax.random.fold_in(splits[4], 71), 0),
        "mean_state": bell_draw(splits[1], (WINDOWS, ROWS), 1.0, 6.0, ((0, 16), (1, 2)), jnp.float32),
        "obs_rows": with_ends(jax.random.randint(splits[2], (WINDOWS, OBS), 0, ROWS_DEV), jax.random.fold_in(splits[2], 1), 0, ROWS_DEV - 1).astype(jnp.int32),
        "obs_precision": jnp.clip(jnp.exp(math.log(0.3125) - 2.3025851 * jax.random.uniform(splits[3], (WINDOWS, OBS), jnp.float32) ** shard_levels(splits[3], (WINDOWS, OBS), ((0, 16), (1, 2)), -0.2, 0.2)), 0.03125, 0.3125),
    }


PRECISE = lax.Precision.HIGHEST

def high_dot(left, right):
    return jnp.dot(left, right, precision=PRECISE, preferred_element_type=jnp.float32)

def inverse_root(gram_matrix):
    unit_matrix = jnp.eye(MEMBERS, dtype=jnp.float32)
    system = unit_matrix + gram_matrix
    frob_scale = jnp.sqrt(jnp.sum(system * system))
    root_iter = system / frob_scale
    inverse = unit_matrix
    for ns_index in range(NS_STEPS):
        factor = 1.5 * unit_matrix - 0.5 * high_dot(inverse, root_iter)
        root_iter = high_dot(root_iter, factor)
        inverse = high_dot(factor, inverse)
    return inverse * (MEMBERS / jnp.trace(inverse))

def window_transform(window_args):
    current, mean_row, row_index, precision = window_args
    obs_block = jnp.arange(OBS, dtype=jnp.int32) // OBS_DEV
    state_index = (obs_block * ROWS_DEV + row_index).astype(jnp.int32)
    picked = jnp.take(current, state_index, axis=0)
    predicted = jnp.tanh(jnp.take(mean_row, state_index)[:, None] + picked)
    centred = (predicted - lax.optimization_barrier(jnp.mean(predicted, axis=1, keepdims=True))) * jnp.sqrt(precision)[:, None]
    gram_matrix = high_dot(centred.T, centred) / (MEMBERS - 1)
    return inverse_root(gram_matrix)

def reference(anomalies, mean_state, obs_rows, obs_precision):
    current = anomalies
    unit_matrix = jnp.eye(MEMBERS, dtype=jnp.float32)
    for sweep_index in range(OUTER):
        transforms = lax.map(window_transform, (current, mean_state, obs_rows, obs_precision))

        def link_window(carry, transform):
            product = high_dot(transform, carry)
            return (product, product)
        unused, carried = lax.scan(link_window, unit_matrix, transforms, reverse=True)
        current = lax.map(lambda window_pair: high_dot(window_pair[0], window_pair[1]), (current, carried))
    return current
```

```python
import functools

import jax
import jax.numpy as jnp
from jax import lax
from jax.experimental import pallas as pl
from jax.experimental.pallas import tpu as pltpu
from jax.sharding import PartitionSpec as P

NS_STEPS = 3
MESH = pl.DeviceIdType.MESH
F32 = jnp.float32
BF16 = jnp.bfloat16


def split2(x):
    hi = x.astype(BF16)
    return hi, (x - hi.astype(F32)).astype(BF16)


def mm(a, b):
    return jnp.dot(a, b, preferred_element_type=F32)


def dot3(a, b):
    (ah, al), (bh, bl) = a, b
    return mm(ah, bh) + (mm(ah, bl) + mm(al, bh))


def column(row, count):
    return jnp.transpose(jnp.broadcast_to(row, (8, count)))[:, :1]


def observed(x_ref, mean_ref, rows_ref, prec_ref):
    rows, members = x_ref.shape[1:]
    obs = rows_ref.shape[1]
    shifted = x_ref[0] + column(mean_ref[...], rows)
    wanted = column(rows_ref[...], obs)
    selector = (lax.broadcasted_iota(jnp.int32, (obs, rows), 1) == wanted).astype(BF16)
    hi = shifted.astype(BF16)
    rest = shifted - hi.astype(F32)
    mid = rest.astype(BF16)
    low = (rest - mid.astype(F32)).astype(BF16)
    predicted = jnp.tanh(mm(selector, hi) + mm(selector, mid) + mm(selector, low))
    centred = predicted - jnp.mean(predicted, axis=1, keepdims=True)
    return centred * jnp.sqrt(column(prec_ref[...], obs))


def gram_of(centred):
    left, right = split2(jnp.transpose(centred)), split2(centred)
    return dot3(left, right)


def inverse_root(gram):
    members = gram.shape[0]
    diagonal = lax.broadcasted_iota(jnp.int32, gram.shape, 0) == lax.broadcasted_iota(
        jnp.int32, gram.shape, 1
    )
    unit = diagonal.astype(F32)
    system = unit + gram
    root = system * (1.0 / jnp.sqrt(jnp.sum(system * system)))
    factor = 1.5 * unit - 0.5 * root
    inverse = split2(factor)
    root = split2(dot3(split2(root), inverse))
    full = None
    for step in range(1, NS_STEPS):
        factor = split2(1.5 * unit - 0.5 * dot3(inverse, root))
        if step + 1 < NS_STEPS:
            root = split2(dot3(root, factor))
        full = dot3(factor, inverse)
        inverse = split2(full)
    return full * (members / jnp.sum(jnp.where(diagonal, full, 0.0)))


def kernel(
    groups, size, parts, x_ref, mean_ref, rows_ref, prec_ref, out_ref,
    c_ref, t_ref, p_ref, v_ref,
    c_send, c_recv, t_send, t_recv, tf_send, tf_recv,
    z_send, z_recv, g_send, g_recv, gf_send, gf_recv,
):
    win, me = lax.axis_index("win"), lax.axis_index("state")
    z, k = win // size, lax.rem(win, size)
    members = x_ref.shape[2]
    share = members // parts
    block = members // (parts * size)

    def remote(ref, send, recv, device):
        return pltpu.make_async_remote_copy(
            src_ref=ref, dst_ref=ref, send_sem=send, recv_sem=recv,
            device_id=device, device_id_type=MESH,
        )

    def sibling(d):
        return win, lax.rem(me + d, parts)

    def peer(d):
        return z * size + lax.rem(k + d, size), me

    barrier = pltpu.get_barrier_semaphore()
    for d in range(1, parts):
        pl.semaphore_signal(barrier, inc=1, device_id=sibling(d), device_id_type=MESH)
    for d in range(1, size):
        pl.semaphore_signal(barrier, inc=1, device_id=peer(d), device_id_type=MESH)
    for d in range(1, groups):
        other = lax.rem(z + d, groups) * size + k
        pl.semaphore_signal(barrier, inc=1, device_id=(other, me), device_id_type=MESH)

    centred = observed(x_ref, mean_ref, rows_ref, prec_ref)
    c_ref[me] = centred
    pl.semaphore_wait(barrier, parts + size + groups - 3)

    sends = []
    for d in range(1, parts):
        copy = remote(c_ref.at[me], c_send.at[d], c_recv.at[me], sibling(d))
        copy.start()
        sends.append(copy)
    gram = gram_of(centred)
    for d in range(1, parts):
        src = lax.rem(me + parts - d, parts)
        remote(c_ref.at[src], c_send.at[d], c_recv.at[src], sibling(d)).wait_recv()
        gram = gram + gram_of(c_ref[src])
    transform = inverse_root(gram * (1.0 / (members - 1)))
    t_ref[k] = transform

    def t_rows(t, part):
        return t_ref.at[t, pl.ds(pl.multiple_of(part * share, share), share), :]

    for d in range(1, size):
        copy = remote(t_rows(k, me), t_send.at[d], t_recv.at[k], peer(d))
        copy.start()
        sends.append(copy)
    v_ref[...] = dot3(split2(x_ref[0]), split2(transform))
    for d in range(1, size):
        src = lax.rem(k + size - d, size)
        remote(t_rows(src, me), t_send.at[d], t_recv.at[src], peer(d)).wait_recv()
        for e in range(1, parts):
            copy = remote(t_rows(src, me), tf_send.at[d, e], tf_recv.at[src, me], sibling(e))
            copy.start()
            sends.append(copy)
    for d in range(1, size):
        src = lax.rem(k + size - d, size)
        for e in range(1, parts):
            part = lax.rem(me + parts - e, parts)
            remote(t_rows(src, part), tf_send.at[d, e], tf_recv.at[src, part], sibling(e)).wait_recv()

    def p_rows(group, index, part):
        first = (index * parts + part) * block
        return p_ref.at[group, pl.ds(pl.multiple_of(first, block), block), :]

    def to_group(d):
        return remote(p_rows(z, k, me), z_send.at[d], z_recv.at[z], ((z - d) * size + k, me))

    @pl.when(z > 0)
    def _():
        first = pl.multiple_of((k * parts + me) * block, block)
        rows = t_ref[0, pl.ds(first, block), :]
        for t in range(1, size):
            rows = dot3(split2(rows), split2(t_ref[t]))
        p_ref[z, pl.ds(first, block), :] = rows

    for d in range(1, groups):
        @pl.when(z >= d)
        def _():
            to_group(d).start()

    for t in range(1, size):
        @pl.when(t > k)
        def _():
            v_ref[...] = dot3(split2(v_ref[...]), split2(t_ref[t]))

    def to_peer(d, e):
        return remote(p_rows(z + d, k, me), g_send.at[d, e], g_recv.at[d, k], peer(e))

    def to_sibling(d, index, e):
        return remote(
            p_rows(z + d, index, me), gf_send.at[d, index, e], gf_recv.at[d, index, me], sibling(e)
        )

    for d in range(1, groups):
        @pl.when(z + d < groups)
        def _():
            remote(p_rows(z + d, k, me), z_send.at[d], z_recv.at[z + d], (win, me)).wait_recv()
            for e in range(1, size):
                to_peer(d, e).start()
            for e in range(1, parts):
                to_sibling(d, k, e).start()

    for d in range(1, groups):
        @pl.when(z + d < groups)
        def _():
            for e in range(1, size):
                src = lax.rem(k + size - e, size)
                remote(
                    p_rows(z + d, src, me), g_send.at[d, e], g_recv.at[d, src], peer(e)
                ).wait_recv()
                for f in range(1, parts):
                    to_sibling(d, src, f).start()

    for d in range(1, groups):
        @pl.when(z + d < groups)
        def _():
            for e in range(1, parts):
                part = lax.rem(me + parts - e, parts)
                for index in range(size):
                    remote(
                        p_rows(z + d, index, part), gf_send.at[d, index, e],
                        gf_recv.at[d, index, part], sibling(e),
                    ).wait_recv()
            v_ref[...] = dot3(split2(v_ref[...]), split2(p_ref[z + d]))

    out_ref[0] = v_ref[...]

    for copy in sends:
        copy.wait_send()
    for d in range(1, groups):
        @pl.when(z >= d)
        def _():
            to_group(d).wait_send()

        @pl.when(z + d < groups)
        def _():
            for e in range(1, size):
                to_peer(d, e).wait_send()
            for e in range(1, parts):
                for index in range(size):
                    to_sibling(d, index, e).wait_send()


def group_size(windows, parts, members):
    size = 1
    while size * size * 4 <= windows and windows % (size * 2) == 0 and members % (16 * size * parts) == 0:
        size *= 2
    return size


def solution(mesh):
    windows, parts = mesh.shape["win"], mesh.shape["state"]

    def shards(anomalies, mean_state, obs_rows, obs_precision):
        rows, members = anomalies.shape[1:]
        obs = obs_rows.shape[1]
        size = group_size(windows, parts, members)
        groups = windows // size
        dma = pltpu.SemaphoreType.DMA
        vmem = pl.BlockSpec(memory_space=pltpu.VMEM)
        return pl.pallas_call(
            functools.partial(kernel, groups, size, parts),
            out_shape=jax.ShapeDtypeStruct(anomalies.shape, F32),
            in_specs=[vmem] * 4,
            out_specs=vmem,
            scratch_shapes=[
                pltpu.VMEM((parts, obs, members), F32),
                pltpu.VMEM((size, members, members), F32),
                pltpu.VMEM((groups, members, members), F32),
                pltpu.VMEM((rows, members), F32),
                dma((parts,)), dma((parts,)),
                dma((size,)), dma((size,)),
                dma((size, parts)), dma((size, parts)),
                dma((groups,)), dma((groups,)),
                dma((groups, size)), dma((groups, size)),
                dma((groups, size, parts)), dma((groups, size, parts)),
            ],
            compiler_params=pltpu.CompilerParams(
                collective_id=0, has_side_effects=True, vmem_limit_bytes=48 * 1024 * 1024
            ),
        )(anomalies, mean_state, obs_rows, obs_precision)

    placed = (P("win", "state", None), P("win", "state"), P("win", "state"), P("win", "state"))
    return jax.shard_map(
        shards, mesh=mesh, in_specs=placed, out_specs=P("win", "state", None), check_vma=False
    )
```

```python
import functools

import jax
import jax.numpy as jnp
from jax import lax
from jax.experimental import pallas as pl
from jax.experimental.pallas import tpu as pltpu
from jax.sharding import PartitionSpec as P

NS_STEPS = 3
MESH = pl.DeviceIdType.MESH
F32 = jnp.float32
BF16 = jnp.bfloat16


def split2(x):
    hi = x.astype(BF16)
    return hi, (x - hi.astype(F32)).astype(BF16)


def mm(a, b):
    return jnp.dot(a, b, preferred_element_type=F32)


def dot3(a, b):
    (ah, al), (bh, bl) = a, b
    return mm(jnp.concatenate([ah, ah, al], axis=1), jnp.concatenate([bh, bl, bh], axis=0))


def column(row, count):
    return jnp.transpose(jnp.broadcast_to(row, (8, count)))[:, :1]


def observed(x_ref, mean_ref, rows_ref, prec_ref):
    rows, members = x_ref.shape
    obs = rows_ref.shape[1]
    shifted = x_ref[...] + column(mean_ref[...], rows)
    wanted = column(rows_ref[...], obs)
    selector = (lax.broadcasted_iota(jnp.int32, (obs, rows), 1) == wanted).astype(BF16)
    hi = shifted.astype(BF16)
    rest = shifted - hi.astype(F32)
    mid = rest.astype(BF16)
    low = (rest - mid.astype(F32)).astype(BF16)
    predicted = jnp.tanh(mm(selector, hi) + mm(selector, mid) + mm(selector, low))
    centred = predicted - jnp.mean(predicted, axis=1, keepdims=True)
    return centred * jnp.sqrt(column(prec_ref[...], obs))


def gram_of(centred):
    left, right = split2(jnp.transpose(centred)), split2(centred)
    return dot3(left, right)


def inverse_root(gram):
    members = gram.shape[0]
    diagonal = lax.broadcasted_iota(jnp.int32, gram.shape, 0) == lax.broadcasted_iota(
        jnp.int32, gram.shape, 1
    )
    unit = diagonal.astype(F32)
    system = unit + gram
    root = system * (1.0 / jnp.sqrt(jnp.sum(system * system)))
    factor = 1.5 * unit - 0.5 * root
    inverse = split2(factor)
    root = split2(dot3(split2(root), inverse))
    full = None
    for step in range(1, NS_STEPS):
        factor = split2(1.5 * unit - 0.5 * dot3(inverse, root))
        if step + 1 < NS_STEPS:
            root = split2(dot3(root, factor))
        full = dot3(factor, inverse)
        inverse = split2(full)
    return full * (members / jnp.sum(jnp.where(diagonal, full, 0.0)))


def kernel(
    groups, size, parts, x_hbm, mean_hbm, rows_hbm, prec_hbm, out_ref,
    x_ref, mean_ref, rows_ref, prec_ref, in_sem, c_ref, t_ref, p_ref, v_ref,
    c_send, c_recv, t_send, t_recv, tf_send, tf_recv,
    z_send, z_recv, g_send, g_recv, gf_send, gf_recv,
):
    win, me = lax.axis_index("win"), lax.axis_index("state")
    z, k = win // size, lax.rem(win, size)
    fetches = [
        pltpu.make_async_copy(src, dst, in_sem.at[i])
        for i, (src, dst) in enumerate(
            [(mean_hbm, mean_ref), (rows_hbm, rows_ref), (prec_hbm, prec_ref), (x_hbm.at[0], x_ref)]
        )
    ]
    for fetch in fetches:
        fetch.start()
    members = x_ref.shape[1]
    share = members // parts
    block = members // (parts * size)

    def remote(ref, send, recv, device):
        return pltpu.make_async_remote_copy(
            src_ref=ref, dst_ref=ref, send_sem=send, recv_sem=recv,
            device_id=device, device_id_type=MESH,
        )

    def sibling(d):
        return win, lax.rem(me + d, parts)

    def peer(d):
        return z * size + lax.rem(k + d, size), me

    barrier = pltpu.get_barrier_semaphore()
    for d in range(1, parts):
        pl.semaphore_signal(barrier, inc=1, device_id=sibling(d), device_id_type=MESH)
    for d in range(1, size):
        pl.semaphore_signal(barrier, inc=1, device_id=peer(d), device_id_type=MESH)
    for d in range(1, groups):
        other = lax.rem(z + d, groups) * size + k
        pl.semaphore_signal(barrier, inc=1, device_id=(other, me), device_id_type=MESH)

    for fetch in fetches:
        fetch.wait()
    centred = observed(x_ref, mean_ref, rows_ref, prec_ref)
    c_ref[me] = centred
    pl.semaphore_wait(barrier, parts + size + groups - 3)

    sends = []
    for d in range(1, parts):
        copy = remote(c_ref.at[me], c_send.at[d], c_recv.at[me], sibling(d))
        copy.start()
        sends.append(copy)
    gram = gram_of(centred)
    for d in range(1, parts):
        src = lax.rem(me + parts - d, parts)
        remote(c_ref.at[src], c_send.at[d], c_recv.at[src], sibling(d)).wait_recv()
        gram = gram + gram_of(c_ref[src])
    transform = inverse_root(gram * (1.0 / (members - 1)))
    t_ref[k] = transform

    def t_rows(t, part):
        return t_ref.at[t, pl.ds(pl.multiple_of(part * share, share), share), :]

    for d in range(1, size):
        copy = remote(t_rows(k, me), t_send.at[d], t_recv.at[k], peer(d))
        copy.start()
        sends.append(copy)
    v_ref[...] = dot3(split2(x_ref[...]), split2(transform))
    for d in range(1, size):
        src = lax.rem(k + size - d, size)
        remote(t_rows(src, me), t_send.at[d], t_recv.at[src], peer(d)).wait_recv()
        for e in range(1, parts):
            copy = remote(t_rows(src, me), tf_send.at[d, e], tf_recv.at[src, me], sibling(e))
            copy.start()
            sends.append(copy)
    for d in range(1, size):
        src = lax.rem(k + size - d, size)
        for e in range(1, parts):
            part = lax.rem(me + parts - e, parts)
            remote(t_rows(src, part), tf_send.at[d, e], tf_recv.at[src, part], sibling(e)).wait_recv()

    def p_rows(group, index, part):
        first = (index * parts + part) * block
        return p_ref.at[group, pl.ds(pl.multiple_of(first, block), block), :]

    def to_group(d):
        return remote(p_rows(z, k, me), z_send.at[d], z_recv.at[z], ((z - d) * size + k, me))

    @pl.when(z > 0)
    def _():
        first = pl.multiple_of((k * parts + me) * block, block)
        rows = t_ref[0, pl.ds(first, block), :]
        for t in range(1, size):
            rows = dot3(split2(rows), split2(t_ref[t]))
        p_ref[z, pl.ds(first, block), :] = rows

    for d in range(1, groups):
        @pl.when(z >= d)
        def _():
            to_group(d).start()

    for t in range(1, size):
        @pl.when(t > k)
        def _():
            v_ref[...] = dot3(split2(v_ref[...]), split2(t_ref[t]))

    def to_peer(d, e):
        return remote(p_rows(z + d, k, me), g_send.at[d, e], g_recv.at[d, k], peer(e))

    def to_sibling(d, index, e):
        return remote(
            p_rows(z + d, index, me), gf_send.at[d, index, e], gf_recv.at[d, index, me], sibling(e)
        )

    for d in range(1, groups):
        @pl.when(z + d < groups)
        def _():
            remote(p_rows(z + d, k, me), z_send.at[d], z_recv.at[z + d], (win, me)).wait_recv()
            for e in range(1, size):
                to_peer(d, e).start()
            for e in range(1, parts):
                to_sibling(d, k, e).start()

    for d in range(1, groups):
        @pl.when(z + d < groups)
        def _():
            for e in range(1, size):
                src = lax.rem(k + size - e, size)
                remote(
                    p_rows(z + d, src, me), g_send.at[d, e], g_recv.at[d, src], peer(e)
                ).wait_recv()
                for f in range(1, parts):
                    to_sibling(d, src, f).start()

    for d in range(1, groups):
        @pl.when(z + d < groups)
        def _():
            for e in range(1, parts):
                part = lax.rem(me + parts - e, parts)
                for index in range(size):
                    remote(
                        p_rows(z + d, index, part), gf_send.at[d, index, e],
                        gf_recv.at[d, index, part], sibling(e),
                    ).wait_recv()
            v_ref[...] = dot3(split2(v_ref[...]), split2(p_ref[z + d]))

    out_ref[0] = v_ref[...]

    for copy in sends:
        copy.wait_send()
    for d in range(1, groups):
        @pl.when(z >= d)
        def _():
            to_group(d).wait_send()

        @pl.when(z + d < groups)
        def _():
            for e in range(1, size):
                to_peer(d, e).wait_send()
            for e in range(1, parts):
                for index in range(size):
                    to_sibling(d, index, e).wait_send()


def group_size(windows, parts, members):
    size = 1
    while size * size * 4 <= windows and windows % (size * 2) == 0 and members % (16 * size * parts) == 0:
        size *= 2
    return size


def solution(mesh):
    windows, parts = mesh.shape["win"], mesh.shape["state"]

    def shards(anomalies, mean_state, obs_rows, obs_precision):
        rows, members = anomalies.shape[1:]
        obs = obs_rows.shape[1]
        size = group_size(windows, parts, members)
        groups = windows // size
        dma = pltpu.SemaphoreType.DMA
        vmem = pl.BlockSpec(memory_space=pltpu.VMEM)
        return pl.pallas_call(
            functools.partial(kernel, groups, size, parts),
            out_shape=jax.ShapeDtypeStruct(anomalies.shape, F32),
            in_specs=[pl.BlockSpec(memory_space=pl.ANY)] * 4,
            out_specs=vmem,
            scratch_shapes=[
                pltpu.VMEM((rows, members), F32),
                pltpu.VMEM((1, rows), F32),
                pltpu.VMEM((1, obs), jnp.int32),
                pltpu.VMEM((1, obs), F32),
                dma((4,)),
                pltpu.VMEM((parts, obs, members), F32),
                pltpu.VMEM((size, members, members), F32),
                pltpu.VMEM((groups, members, members), F32),
                pltpu.VMEM((rows, members), F32),
                dma((parts,)), dma((parts,)),
                dma((size,)), dma((size,)),
                dma((size, parts)), dma((size, parts)),
                dma((groups,)), dma((groups,)),
                dma((groups, size)), dma((groups, size)),
                dma((groups, size, parts)), dma((groups, size, parts)),
            ],
            compiler_params=pltpu.CompilerParams(
                collective_id=0, has_side_effects=True, vmem_limit_bytes=56 * 1024 * 1024
            ),
        )(anomalies, mean_state, obs_rows, obs_precision)

    placed = (P("win", "state", None), P("win", "state"), P("win", "state"), P("win", "state"))
    return jax.shard_map(
        shards, mesh=mesh, in_specs=placed, out_specs=P("win", "state", None), check_vma=False
    )
```

```python
import functools

import jax
import jax.numpy as jnp
from jax import lax
from jax.experimental import pallas as pl
from jax.experimental.pallas import tpu as pltpu
from jax.sharding import PartitionSpec as P

NS_STEPS = 3
MESH = pl.DeviceIdType.MESH
F32 = jnp.float32
BF16 = jnp.bfloat16


def split2(x):
    hi = x.astype(BF16)
    return hi, (x - hi.astype(F32)).astype(BF16)


def mm(a, b):
    return jnp.dot(a, b, preferred_element_type=F32)


def dot3(a, b):
    (ah, al), (bh, bl) = a, b
    return mm(jnp.concatenate([ah, ah, al], axis=1), jnp.concatenate([bh, bl, bh], axis=0))


def column(row, count):
    return jnp.transpose(jnp.broadcast_to(row, (8, count)))[:, :1]


def observed(x_ref, mean_ref, rows_ref, prec_ref):
    rows, members = x_ref.shape
    obs = rows_ref.shape[1]
    shifted = x_ref[...] + column(mean_ref[...], rows)
    wanted = column(rows_ref[...], obs)
    selector = (lax.broadcasted_iota(jnp.int32, (obs, rows), 1) == wanted).astype(BF16)
    hi = shifted.astype(BF16)
    rest = shifted - hi.astype(F32)
    mid = rest.astype(BF16)
    low = (rest - mid.astype(F32)).astype(BF16)
    predicted = jnp.tanh(mm(selector, hi) + mm(selector, mid) + mm(selector, low))
    centred = predicted - jnp.mean(predicted, axis=1, keepdims=True)
    return centred * jnp.sqrt(column(prec_ref[...], obs))


def gram_of(centred):
    left, right = split2(jnp.transpose(centred)), split2(centred)
    return dot3(left, right)


def inverse_root(gram):
    members = gram.shape[0]
    diagonal = lax.broadcasted_iota(jnp.int32, gram.shape, 0) == lax.broadcasted_iota(
        jnp.int32, gram.shape, 1
    )
    unit = diagonal.astype(F32)
    system = unit + gram
    root = system * (1.0 / jnp.sqrt(jnp.sum(system * system)))
    factor = 1.5 * unit - 0.5 * root
    inverse = split2(factor)
    root = split2(dot3(split2(root), inverse))
    full = None
    for step in range(1, NS_STEPS):
        factor = split2(1.5 * unit - 0.5 * dot3(inverse, root))
        if step + 1 < NS_STEPS:
            root = split2(dot3(root, factor))
        full = dot3(factor, inverse)
        inverse = split2(full)
    return full * (members / jnp.sum(jnp.where(diagonal, full, 0.0)))


def flipped(index, bits):
    result, bit = index, 1
    while bit <= bits:
        if bits & bit:
            result = result + bit * (1 - 2 * lax.rem(index // bit, 2))
        bit *= 2
    return result


def positions(half):
    return (
        lax.broadcasted_iota(jnp.int32, (half, half), 0),
        lax.broadcasted_iota(jnp.int32, (half, half), 1),
    )


def pack(matrix, ref, slot):
    half, parts, share = matrix.shape[0] // 2, ref.shape[1], ref.shape[2] - 8
    r, c = positions(half)
    upper, lower = matrix[:half, :half], matrix[half:, half:]
    both = jnp.where(r <= c, upper, lower)
    diagonal = jnp.sum(jnp.where(r == c, lower, 0.0), axis=0, keepdims=True)
    tail = jnp.broadcast_to(jnp.concatenate([diagonal, diagonal], axis=1), (8, 2 * half))
    for part in range(parts):
        rows = slice(part * share, (part + 1) * share)
        ref[slot, part, :share, :half] = both[rows]
        ref[slot, part, :share, half:] = matrix[rows, half:]
        ref[slot, part, share:, :] = tail


def unpacked(ref, slot):
    parts, share, half = ref.shape[1], ref.shape[2] - 8, ref.shape[3] // 2
    r, c = positions(half)
    rows = jnp.concatenate([ref[slot, part, :share, :] for part in range(parts)], axis=0)
    both, right = rows[:, :half], rows[:, half:]
    turned = jnp.transpose(both)
    diagonal = ref[slot, 0, share : share + 1, :half]
    upper = jnp.where(r <= c, both, turned)
    lower = jnp.where(r > c, both, jnp.where(r == c, diagonal, turned))
    return jnp.concatenate(
        [
            jnp.concatenate([upper, right], axis=1),
            jnp.concatenate([jnp.transpose(right), lower], axis=1),
        ],
        axis=0,
    )


def kernel(
    groups, size, parts, x_hbm, mean_hbm, rows_hbm, prec_hbm, out_ref,
    x_ref, mean_ref, rows_ref, prec_ref, in_sem, c_ref, tp_ref, t_ref, th_ref, tl_ref, p_ref, v_ref,
    c_send, c_recv, t_send, t_recv, tf_send, tf_recv,
    z_send, z_recv, g_send, g_recv, gf_send, gf_recv,
):
    win, me = lax.axis_index("win"), lax.axis_index("state")
    z, k = win // size, lax.rem(win, size)
    fetches = [
        pltpu.make_async_copy(src, dst, in_sem.at[i])
        for i, (src, dst) in enumerate(
            [(mean_hbm, mean_ref), (rows_hbm, rows_ref), (prec_hbm, prec_ref), (x_hbm.at[0], x_ref)]
        )
    ]
    for fetch in fetches:
        fetch.start()
    members = x_ref.shape[1]
    block = members // (parts * size)

    def remote(ref, send, recv, device):
        return pltpu.make_async_remote_copy(
            src_ref=ref, dst_ref=ref, send_sem=send, recv_sem=recv,
            device_id=device, device_id_type=MESH,
        )

    def sibling(d):
        return win, lax.rem(me + d, parts)

    def peer(d):
        return z * size + flipped(k, d), me

    barrier = pltpu.get_barrier_semaphore()
    for d in range(1, parts):
        pl.semaphore_signal(barrier, inc=1, device_id=sibling(d), device_id_type=MESH)
    for d in range(1, size):
        pl.semaphore_signal(barrier, inc=1, device_id=peer(d), device_id_type=MESH)
    for d in range(1, groups):
        other = lax.rem(z + d, groups) * size + k
        pl.semaphore_signal(barrier, inc=1, device_id=(other, me), device_id_type=MESH)

    for fetch in fetches:
        fetch.wait()
    centred = observed(x_ref, mean_ref, rows_ref, prec_ref)
    c_ref[me] = centred
    pl.semaphore_wait(barrier, parts + size + groups - 3)

    sends = []
    for d in range(1, parts):
        copy = remote(c_ref.at[me], c_send.at[d], c_recv.at[me], sibling(d))
        copy.start()
        sends.append(copy)
    gram = gram_of(centred)
    for d in range(1, parts):
        src = lax.rem(me + parts - d, parts)
        remote(c_ref.at[src], c_send.at[d], c_recv.at[src], sibling(d)).wait_recv()
        gram = gram + gram_of(c_ref[src])
    transform = inverse_root(gram * (1.0 / (members - 1)))
    pack(transform, tp_ref, k)

    def t_share(t, part):
        return tp_ref.at[t, part]

    for d in range(1, size):
        copy = remote(t_share(k, me), t_send.at[d], t_recv.at[d], peer(d))
        copy.start()
        sends.append(copy)
    own = split2(transform)
    t_ref[k], th_ref[k], tl_ref[k] = transform, own[0], own[1]
    v_ref[...] = dot3(split2(x_ref[...]), own)
    for d in range(1, size):
        src = flipped(k, d)
        remote(t_share(src, me), t_send.at[d], t_recv.at[d], peer(d)).wait_recv()
        for e in range(1, parts):
            copy = remote(t_share(src, me), tf_send.at[d, e], tf_recv.at[d, me], sibling(e))
            copy.start()
            sends.append(copy)
    for d in range(1, size):
        src = flipped(k, d)
        for e in range(1, parts):
            part = lax.rem(me + parts - e, parts)
            remote(t_share(src, part), tf_send.at[d, e], tf_recv.at[d, part], sibling(e)).wait_recv()
        received = unpacked(tp_ref, src)
        t_ref[src] = received
        th_ref[src], tl_ref[src] = split2(received)

    def p_rows(group, index):
        return p_ref.at[group, me, pl.ds(pl.multiple_of(index * block, block), block), :]

    def to_group(d):
        return remote(p_rows(z, k), z_send.at[d], z_recv.at[d], ((z - d) * size + k, me))

    @pl.when(z > 0)
    def _():
        first = pl.multiple_of((me * size + k) * block, block)
        rows = t_ref[0, pl.ds(first, block), :]
        for t in range(1, size):
            rows = dot3(split2(rows), (th_ref[t], tl_ref[t]))
        p_ref[z, me, pl.ds(pl.multiple_of(k * block, block), block), :] = rows

    for d in range(1, groups):
        @pl.when(z >= d)
        def _():
            to_group(d).start()

    for t in range(1, size):
        @pl.when(t > k)
        def _():
            v_ref[...] = dot3(split2(v_ref[...]), (th_ref[t], tl_ref[t]))

    def to_peer(d, e):
        return remote(p_rows(z + d, k), g_send.at[d, e], g_recv.at[d, e], peer(e))

    def to_sibling(d, e):
        return remote(p_ref.at[z + d, me], gf_send.at[d, e], gf_recv.at[d, me], sibling(e))

    def finish(d):
        for e in range(1, parts):
            part = lax.rem(me + parts - e, parts)
            remote(
                p_ref.at[z + d, part], gf_send.at[d, e], gf_recv.at[d, part], sibling(e)
            ).wait_recv()
        product = jnp.concatenate([p_ref[z + d, part] for part in range(parts)], axis=0)
        v_ref[...] = dot3(split2(v_ref[...]), split2(product))

    for d in range(1, groups):
        @pl.when(z + d < groups)
        def _():
            remote(p_rows(z + d, k), z_send.at[d], z_recv.at[d], (win, me)).wait_recv()
            for e in range(1, size):
                to_peer(d, e).start()

    for d in range(1, groups):
        @pl.when(z + d < groups)
        def _():
            for e in range(1, size):
                src = flipped(k, e)
                remote(p_rows(z + d, src), g_send.at[d, e], g_recv.at[d, e], peer(e)).wait_recv()
            for e in range(1, parts):
                to_sibling(d, e).start()
            if d > 1:
                finish(d - 1)

        @pl.when(z + d == groups - 1)
        def _():
            finish(d)

    out_ref[0] = v_ref[...]

    for copy in sends:
        copy.wait_send()
    for d in range(1, groups):
        @pl.when(z >= d)
        def _():
            to_group(d).wait_send()

        @pl.when(z + d < groups)
        def _():
            for e in range(1, size):
                to_peer(d, e).wait_send()
            for e in range(1, parts):
                to_sibling(d, e).wait_send()


def group_size(windows, parts, members):
    size = 1
    while size * size * 4 <= windows and windows % (size * 2) == 0 and members % (16 * size * parts) == 0:
        size *= 2
    return size


def solution(mesh):
    windows, parts = mesh.shape["win"], mesh.shape["state"]

    def shards(anomalies, mean_state, obs_rows, obs_precision):
        rows, members = anomalies.shape[1:]
        obs = obs_rows.shape[1]
        size = group_size(windows, parts, members)
        groups = windows // size
        dma = pltpu.SemaphoreType.DMA
        vmem = pl.BlockSpec(memory_space=pltpu.VMEM)
        return pl.pallas_call(
            functools.partial(kernel, groups, size, parts),
            out_shape=jax.ShapeDtypeStruct(anomalies.shape, F32),
            in_specs=[pl.BlockSpec(memory_space=pltpu.HBM)] * 4,
            out_specs=vmem,
            scratch_shapes=[
                pltpu.VMEM((rows, members), F32),
                pltpu.VMEM((1, rows), F32),
                pltpu.VMEM((1, obs), jnp.int32),
                pltpu.VMEM((1, obs), F32),
                dma((4,)),
                pltpu.VMEM((parts, obs, members), F32),
                pltpu.VMEM((size, parts, members // (2 * parts) + 8, members), F32),
                pltpu.VMEM((size, members, members), F32),
                pltpu.VMEM((size, members, members), BF16),
                pltpu.VMEM((size, members, members), BF16),
                pltpu.VMEM((groups, parts, members // parts, members), F32),
                pltpu.VMEM((rows, members), F32),
                dma((parts,)), dma((parts,)),
                dma((size,)), dma((size,)),
                dma((size, parts)), dma((size, parts)),
                dma((groups,)), dma((groups,)),
                dma((groups, size)), dma((groups, size)),
                dma((groups, parts)), dma((groups, parts)),
            ],
            compiler_params=pltpu.CompilerParams(
                collective_id=0, has_side_effects=True, vmem_limit_bytes=56 * 1024 * 1024
            ),
        )(anomalies, mean_state, obs_rows, obs_precision)

    placed = (P("win", "state", None), P("win", "state"), P("win", "state"), P("win", "state"))
    return jax.shard_map(
        shards, mesh=mesh, in_specs=placed, out_specs=P("win", "state", None), check_vma=False
    )
```

```python
import functools

import jax
import jax.numpy as jnp
from jax import lax
from jax.experimental import pallas as pl
from jax.experimental.pallas import tpu as pltpu
from jax.sharding import PartitionSpec as P

NS_STEPS = 3
MESH = pl.DeviceIdType.MESH
F32 = jnp.float32
BF16 = jnp.bfloat16


def split2(x):
    hi = x.astype(BF16)
    return hi, (x - hi.astype(F32)).astype(BF16)


def mm(a, b):
    return jnp.dot(a, b, preferred_element_type=F32)


def dot3(a, b):
    (ah, al), (bh, bl) = a, b
    return mm(jnp.concatenate([ah, ah, al], axis=1), jnp.concatenate([bh, bl, bh], axis=0))


def column(row, count):
    return jnp.transpose(jnp.broadcast_to(row, (8, count)))[:, :1]


def observed(x_ref, mean_ref, rows_ref, prec_ref):
    rows, members = x_ref.shape
    obs = rows_ref.shape[1]
    shifted = x_ref[...] + column(mean_ref[...], rows)
    wanted = column(rows_ref[...], obs)
    selector = (lax.broadcasted_iota(jnp.int32, (obs, rows), 1) == wanted).astype(BF16)
    hi = shifted.astype(BF16)
    rest = shifted - hi.astype(F32)
    mid = rest.astype(BF16)
    low = (rest - mid.astype(F32)).astype(BF16)
    predicted = jnp.tanh(mm(selector, hi) + mm(selector, mid) + mm(selector, low))
    centred = predicted - jnp.mean(predicted, axis=1, keepdims=True)
    return centred * jnp.sqrt(column(prec_ref[...], obs))


def gram_of(centred):
    left, right = split2(jnp.transpose(centred)), split2(centred)
    return dot3(left, right)


def inverse_root(gram):
    members = gram.shape[0]
    diagonal = lax.broadcasted_iota(jnp.int32, gram.shape, 0) == lax.broadcasted_iota(
        jnp.int32, gram.shape, 1
    )
    unit = diagonal.astype(F32)
    system = unit + gram
    root = system * (1.0 / jnp.sqrt(jnp.sum(system * system)))
    factor = 1.5 * unit - 0.5 * root
    inverse = split2(factor)
    root = split2(dot3(split2(root), inverse))
    full = None
    for step in range(1, NS_STEPS):
        factor = split2(1.5 * unit - 0.5 * dot3(inverse, root))
        if step + 1 < NS_STEPS:
            root = split2(dot3(root, factor))
        full = dot3(factor, inverse)
        inverse = split2(full)
    return full * (members / jnp.sum(jnp.where(diagonal, full, 0.0)))


def flipped(index, bits):
    result, bit = index, 1
    while bit <= bits:
        if bits & bit:
            result = result + bit * (1 - 2 * lax.rem(index // bit, 2))
        bit *= 2
    return result


def positions(half):
    return (
        lax.broadcasted_iota(jnp.int32, (half, half), 0),
        lax.broadcasted_iota(jnp.int32, (half, half), 1),
    )


def pack(matrix, ref, slot):
    half, parts, share = matrix.shape[0] // 2, ref.shape[1], ref.shape[2] - 8
    r, c = positions(half)
    upper, lower = matrix[:half, :half], matrix[half:, half:]
    both = jnp.where(r <= c, upper, lower)
    diagonal = jnp.sum(jnp.where(r == c, lower, 0.0), axis=0, keepdims=True)
    tail = jnp.broadcast_to(jnp.concatenate([diagonal, diagonal], axis=1), (8, 2 * half))
    for part in range(parts):
        rows = slice(part * share, (part + 1) * share)
        ref[slot, part, :share, :half] = both[rows]
        ref[slot, part, :share, half:] = matrix[rows, half:]
        ref[slot, part, share:, :] = tail


def unpacked(ref, slot):
    parts, share, half = ref.shape[1], ref.shape[2] - 8, ref.shape[3] // 2
    r, c = positions(half)
    rows = jnp.concatenate([ref[slot, part, :share, :] for part in range(parts)], axis=0)
    both, right = rows[:, :half], rows[:, half:]
    turned = jnp.transpose(both)
    diagonal = ref[slot, 0, share : share + 1, :half]
    upper = jnp.where(r <= c, both, turned)
    lower = jnp.where(r > c, both, jnp.where(r == c, diagonal, turned))
    return jnp.concatenate(
        [
            jnp.concatenate([upper, right], axis=1),
            jnp.concatenate([jnp.transpose(right), lower], axis=1),
        ],
        axis=0,
    )


def kernel(
    groups, size, parts, x_hbm, mean_hbm, rows_hbm, prec_hbm, out_ref,
    x_ref, mean_ref, rows_ref, prec_ref, in_sem, c_ref, tp_ref, t_ref, th_ref, tl_ref, p_ref, v_ref,
    c_send, c_recv, t_send, t_recv, tf_send, tf_recv,
    z_send, z_recv, g_send, g_recv, gf_send, gf_recv,
):
    win, me = lax.axis_index("win"), lax.axis_index("state")
    z, k = win // size, lax.rem(win, size)
    fetches = [
        pltpu.make_async_copy(src, dst, in_sem.at[i])
        for i, (src, dst) in enumerate(
            [(mean_hbm, mean_ref), (rows_hbm, rows_ref), (prec_hbm, prec_ref), (x_hbm.at[0], x_ref)]
        )
    ]
    for fetch in fetches:
        fetch.start()
    members = x_ref.shape[1]
    block = members // (parts * size)

    def remote(ref, send, recv, device):
        return pltpu.make_async_remote_copy(
            src_ref=ref, dst_ref=ref, send_sem=send, recv_sem=recv,
            device_id=device, device_id_type=MESH,
        )

    def sibling(d):
        return win, lax.rem(me + d, parts)

    def peer(d):
        return z * size + flipped(k, d), me

    barrier = pltpu.get_barrier_semaphore()
    for e in range(1, parts):
        pl.semaphore_signal(barrier, inc=1, device_id=sibling(e), device_id_type=MESH)
    for e in range(parts):
        part = lax.rem(me + e, parts)
        for d in range(1, size):
            device = (z * size + flipped(k, d), part)
            pl.semaphore_signal(barrier, inc=1, device_id=device, device_id_type=MESH)
        for d in range(1, groups):
            device = (lax.rem(z + d, groups) * size + k, part)
            pl.semaphore_signal(barrier, inc=1, device_id=device, device_id_type=MESH)

    for fetch in fetches:
        fetch.wait()
    centred = observed(x_ref, mean_ref, rows_ref, prec_ref)
    c_ref[me] = centred
    pl.semaphore_wait(barrier, parts - 1 + parts * (size + groups - 2))

    sends = []
    for d in range(1, parts):
        copy = remote(c_ref.at[me], c_send.at[d], c_recv.at[me], sibling(d))
        copy.start()
        sends.append(copy)
    gram = gram_of(centred)
    for d in range(1, parts):
        src = lax.rem(me + parts - d, parts)
        remote(c_ref.at[src], c_send.at[d], c_recv.at[src], sibling(d)).wait_recv()
        gram = gram + gram_of(c_ref[src])
    transform = inverse_root(gram * (1.0 / (members - 1)))
    pack(transform, tp_ref, k)

    def to_lead(d, part):
        return remote(
            tp_ref.at[k, part], t_send.at[d], t_recv.at[d, part], (z * size + flipped(k, d), 0)
        )

    def from_lead(d, e):
        return remote(
            tp_ref.at[flipped(k, d)], tf_send.at[d, e], tf_recv.at[d], (win, e)
        )

    def keep(d):
        src = flipped(k, d)
        received = unpacked(tp_ref, src)
        t_ref[src] = received
        th_ref[src], tl_ref[src] = split2(received)

    for d in range(1, size):
        copy = to_lead(d, me)
        copy.start()
        sends.append(copy)
    own = split2(transform)
    t_ref[k], th_ref[k], tl_ref[k] = transform, own[0], own[1]
    v_ref[...] = dot3(split2(x_ref[...]), own)

    def p_rows(group, part, index):
        return p_ref.at[group, part, pl.ds(pl.multiple_of(index * block, block), block), :]

    def to_group(d, part):
        return remote(
            p_rows(z, part, k), z_send.at[d, part], z_recv.at[d], ((z - d) * size + k, part)
        )

    @pl.when(me == 0)
    def _():
        for d in range(1, size):
            src = flipped(k, d)
            for part in range(parts):
                remote(
                    tp_ref.at[src, part], t_send.at[d], t_recv.at[d, part], (win, me)
                ).wait_recv()
            for e in range(1, parts):
                from_lead(d, e).start()
            keep(d)

        @pl.when(z > 0)
        def _():
            rows = jnp.concatenate(
                [
                    t_ref[0, pl.ds(pl.multiple_of((part * size + k) * block, block), block), :]
                    for part in range(parts)
                ],
                axis=0,
            )
            for t in range(1, size):
                rows = dot3(split2(rows), (th_ref[t], tl_ref[t]))
            for part in range(parts):
                p_ref[z, part, pl.ds(pl.multiple_of(k * block, block), block), :] = rows[
                    part * block : (part + 1) * block
                ]

        for d in reversed(range(1, groups)):
            @pl.when(z >= d)
            def _():
                for part in range(parts):
                    to_group(d, part).start()

    @pl.when(me > 0)
    def _():
        for d in range(1, size):
            remote(tp_ref.at[flipped(k, d)], t_send.at[d], tf_recv.at[d], (win, me)).wait_recv()
            keep(d)

    for t in range(1, size):
        @pl.when(t > k)
        def _():
            v_ref[...] = dot3(split2(v_ref[...]), (th_ref[t], tl_ref[t]))

    def to_peer(d, e):
        return remote(p_rows(z + d, me, k), g_send.at[d, e], g_recv.at[d, e], peer(e))

    def to_sibling(d, e):
        return remote(p_ref.at[z + d, me], gf_send.at[d, e], gf_recv.at[d, me], sibling(e))

    def spread(d):
        remote(p_rows(z + d, me, k), z_send.at[d, 0], z_recv.at[d], (win, me)).wait_recv()
        for e in reversed(range(1, size)):
            to_peer(d, e).start()

    def share(d):
        for e in range(1, size):
            remote(
                p_rows(z + d, me, flipped(k, e)), g_send.at[d, e], g_recv.at[d, e], peer(e)
            ).wait_recv()
        for e in range(1, parts):
            to_sibling(d, e).start()

    def finish(d):
        for e in range(1, parts):
            part = lax.rem(me + parts - e, parts)
            remote(
                p_ref.at[z + d, part], gf_send.at[d, e], gf_recv.at[d, part], sibling(e)
            ).wait_recv()
        product = jnp.concatenate([p_ref[z + d, part] for part in range(parts)], axis=0)
        v_ref[...] = dot3(split2(v_ref[...]), split2(product))

    for step in range(1, groups + 2):
        for late, stage in enumerate((spread, share, finish)):
            if 1 <= step - late < groups:
                pl.when(z + step - late < groups)(functools.partial(stage, step - late))

    out_ref[0] = v_ref[...]

    for copy in sends:
        copy.wait_send()

    @pl.when(me == 0)
    def _():
        for d in range(1, size):
            for e in range(1, parts):
                from_lead(d, e).wait_send()
        for d in range(1, groups):
            @pl.when(z >= d)
            def _():
                for part in range(parts):
                    to_group(d, part).wait_send()

    for d in range(1, groups):
        @pl.when(z + d < groups)
        def _():
            for e in range(1, size):
                to_peer(d, e).wait_send()
            for e in range(1, parts):
                to_sibling(d, e).wait_send()


def group_size(windows, parts, members):
    size = 1
    while size * size * 4 <= windows and windows % (size * 2) == 0 and members % (16 * size * parts) == 0:
        size *= 2
    return size


def solution(mesh):
    windows, parts = mesh.shape["win"], mesh.shape["state"]

    def shards(anomalies, mean_state, obs_rows, obs_precision):
        rows, members = anomalies.shape[1:]
        obs = obs_rows.shape[1]
        size = group_size(windows, parts, members)
        groups = windows // size
        dma = pltpu.SemaphoreType.DMA
        vmem = pl.BlockSpec(memory_space=pltpu.VMEM)
        return pl.pallas_call(
            functools.partial(kernel, groups, size, parts),
            out_shape=pltpu.VMEM(anomalies.shape, F32),
            in_specs=[pl.BlockSpec(memory_space=pltpu.HBM)] * 4,
            out_specs=vmem,
            scratch_shapes=[
                pltpu.VMEM((rows, members), F32),
                pltpu.VMEM((1, rows), F32),
                pltpu.VMEM((1, obs), jnp.int32),
                pltpu.VMEM((1, obs), F32),
                dma((4,)),
                pltpu.VMEM((parts, obs, members), F32),
                pltpu.VMEM((size, parts, members // (2 * parts) + 8, members), F32),
                pltpu.VMEM((size, members, members), F32),
                pltpu.VMEM((size, members, members), BF16),
                pltpu.VMEM((size, members, members), BF16),
                pltpu.VMEM((groups, parts, members // parts, members), F32),
                pltpu.VMEM((rows, members), F32),
                dma((parts,)), dma((parts,)),
                dma((size,)), dma((size, parts)),
                dma((size, parts)), dma((size,)),
                dma((groups, parts)), dma((groups,)),
                dma((groups, size)), dma((groups, size)),
                dma((groups, parts)), dma((groups, parts)),
            ],
            compiler_params=pltpu.CompilerParams(
                collective_id=0, has_side_effects=True, vmem_limit_bytes=56 * 1024 * 1024
            ),
        )(anomalies, mean_state, obs_rows, obs_precision)

    placed = (P("win", "state", None), P("win", "state"), P("win", "state"), P("win", "state"))
    return jax.shard_map(
        shards, mesh=mesh, in_specs=placed, out_specs=P("win", "state", None), check_vma=False
    )
```

```python
import functools

import jax
import jax.numpy as jnp
from jax import lax
from jax.experimental import pallas as pl
from jax.experimental.pallas import tpu as pltpu
from jax.sharding import PartitionSpec as P

NS_STEPS = 3
MESH = pl.DeviceIdType.MESH
F32 = jnp.float32
BF16 = jnp.bfloat16


def split2(x):
    hi = x.astype(BF16)
    return hi, (x - hi.astype(F32)).astype(BF16)


def mm(a, b):
    return jnp.dot(a, b, preferred_element_type=F32)


def dot3(a, b):
    (ah, al), (bh, bl) = a, b
    return mm(jnp.concatenate([ah, ah, al], axis=1), jnp.concatenate([bh, bl, bh], axis=0))


def column(row, count):
    return jnp.transpose(jnp.broadcast_to(row, (8, count)))[:, :1]


def observed(x_ref, mean_ref, rows_ref, prec_ref):
    rows, members = x_ref.shape
    obs = rows_ref.shape[1]
    shifted = x_ref[...] + column(mean_ref[...], rows)
    wanted = column(rows_ref[...], obs)
    selector = (lax.broadcasted_iota(jnp.int32, (obs, rows), 1) == wanted).astype(BF16)
    hi = shifted.astype(BF16)
    rest = shifted - hi.astype(F32)
    mid = rest.astype(BF16)
    low = (rest - mid.astype(F32)).astype(BF16)
    predicted = jnp.tanh(mm(selector, hi) + mm(selector, mid) + mm(selector, low))
    centred = predicted - jnp.mean(predicted, axis=1, keepdims=True)
    return centred * jnp.sqrt(column(prec_ref[...], obs))


def gram_of(centred):
    left, right = split2(jnp.transpose(centred)), split2(centred)
    return dot3(left, right)


def inverse_root(gram):
    members = gram.shape[0]
    diagonal = lax.broadcasted_iota(jnp.int32, gram.shape, 0) == lax.broadcasted_iota(
        jnp.int32, gram.shape, 1
    )
    unit = diagonal.astype(F32)
    system = unit + gram
    root = system * (1.0 / jnp.sqrt(jnp.sum(system * system)))
    factor = 1.5 * unit - 0.5 * root
    inverse = split2(factor)
    root = split2(dot3(split2(root), inverse))
    full = None
    for step in range(1, NS_STEPS):
        factor = split2(1.5 * unit - 0.5 * dot3(inverse, root))
        if step + 1 < NS_STEPS:
            root = split2(dot3(root, factor))
        full = dot3(factor, inverse)
        inverse = split2(full)
    return full * (members / jnp.sum(jnp.where(diagonal, full, 0.0)))


def flipped(index, bits):
    result, bit = index, 1
    while bit <= bits:
        if bits & bit:
            result = result + bit * (1 - 2 * lax.rem(index // bit, 2))
        bit *= 2
    return result


def positions(half):
    return (
        lax.broadcasted_iota(jnp.int32, (half, half), 0),
        lax.broadcasted_iota(jnp.int32, (half, half), 1),
    )


def pack(matrix, ref, slot):
    half, parts, share = matrix.shape[0] // 2, ref.shape[1], ref.shape[2] - 8
    r, c = positions(half)
    upper, lower = matrix[:half, :half], matrix[half:, half:]
    both = jnp.where(r <= c, upper, lower)
    diagonal = jnp.sum(jnp.where(r == c, lower, 0.0), axis=0, keepdims=True)
    tail = jnp.broadcast_to(jnp.concatenate([diagonal, diagonal], axis=1), (8, 2 * half))
    for part in range(parts):
        rows = slice(part * share, (part + 1) * share)
        ref[slot, part, :share, :half] = both[rows]
        ref[slot, part, :share, half:] = matrix[rows, half:]
        ref[slot, part, share:, :] = tail


def unpacked(ref, slot):
    parts, share, half = ref.shape[1], ref.shape[2] - 8, ref.shape[3] // 2
    r, c = positions(half)
    rows = jnp.concatenate([ref[slot, part, :share, :] for part in range(parts)], axis=0)
    both, right = rows[:, :half], rows[:, half:]
    turned = jnp.transpose(both)
    diagonal = ref[slot, 0, share : share + 1, :half]
    upper = jnp.where(r <= c, both, turned)
    lower = jnp.where(r > c, both, jnp.where(r == c, diagonal, turned))
    return jnp.concatenate(
        [
            jnp.concatenate([upper, right], axis=1),
            jnp.concatenate([jnp.transpose(right), lower], axis=1),
        ],
        axis=0,
    )


def kernel(
    groups, size, parts, x_hbm, mean_hbm, rows_hbm, prec_hbm, out_ref,
    x_ref, mean_ref, rows_ref, prec_ref, in_sem, c_ref, tp_ref, t_ref, th_ref, tl_ref, p_ref, v_ref,
    c_send, c_recv, t_send, t_recv, tf_send, tf_recv,
    z_send, z_recv, zf_send, zf_recv, g_send, g_recv, gf_send, gf_recv,
):
    win, me = lax.axis_index("win"), lax.axis_index("state")
    z, k = win // size, lax.rem(win, size)
    fetches = [
        pltpu.make_async_copy(src, dst, in_sem.at[i])
        for i, (src, dst) in enumerate(
            [(mean_hbm, mean_ref), (rows_hbm, rows_ref), (prec_hbm, prec_ref), (x_hbm.at[0], x_ref)]
        )
    ]
    for fetch in fetches:
        fetch.start()
    members = x_ref.shape[1]
    block = members // (parts * size)

    def remote(ref, send, recv, device):
        return pltpu.make_async_remote_copy(
            src_ref=ref, dst_ref=ref, send_sem=send, recv_sem=recv,
            device_id=device, device_id_type=MESH,
        )

    def sibling(d):
        return win, lax.rem(me + d, parts)

    def peer(d):
        return z * size + flipped(k, d), me

    barrier = pltpu.get_barrier_semaphore()
    for e in range(1, parts):
        pl.semaphore_signal(barrier, inc=1, device_id=sibling(e), device_id_type=MESH)
    for e in range(parts):
        part = lax.rem(me + e, parts)
        for d in range(1, size):
            device = (z * size + flipped(k, d), part)
            pl.semaphore_signal(barrier, inc=1, device_id=device, device_id_type=MESH)
        for d in range(1, groups):
            device = (lax.rem(z + d, groups) * size + k, part)
            pl.semaphore_signal(barrier, inc=1, device_id=device, device_id_type=MESH)

    for fetch in fetches:
        fetch.wait()
    centred = observed(x_ref, mean_ref, rows_ref, prec_ref)
    c_ref[me] = centred
    pl.semaphore_wait(barrier, parts - 1 + parts * (size + groups - 2))

    sends = []
    for d in range(1, parts):
        copy = remote(c_ref.at[me], c_send.at[d], c_recv.at[me], sibling(d))
        copy.start()
        sends.append(copy)
    gram = gram_of(centred)
    for d in range(1, parts):
        src = lax.rem(me + parts - d, parts)
        remote(c_ref.at[src], c_send.at[d], c_recv.at[src], sibling(d)).wait_recv()
        gram = gram + gram_of(c_ref[src])
    transform = inverse_root(gram * (1.0 / (members - 1)))
    pack(transform, tp_ref, k)

    def to_lead(d, part):
        return remote(
            tp_ref.at[k, part], t_send.at[d], t_recv.at[d, part], (z * size + flipped(k, d), 0)
        )

    def from_lead(d, e):
        return remote(
            tp_ref.at[flipped(k, d)], tf_send.at[d, e], tf_recv.at[d], (win, e)
        )

    def keep(d):
        src = flipped(k, d)
        received = unpacked(tp_ref, src)
        t_ref[src] = received
        th_ref[src], tl_ref[src] = split2(received)

    for d in range(1, size):
        copy = to_lead(d, me)
        copy.start()
        sends.append(copy)
    own = split2(transform)
    t_ref[k], th_ref[k], tl_ref[k] = transform, own[0], own[1]
    v_ref[...] = dot3(split2(x_ref[...]), own)

    def p_rows(group, part, index):
        return p_ref.at[group, part, pl.ds(pl.multiple_of(index * block, block), block), :]

    def to_group(d, part):
        return remote(
            p_rows(z, part, k), z_send.at[d, part], z_recv.at[d], ((z - d) * size + k, part)
        )

    far = flipped(k, size - 1)

    def to_first(part):
        return remote(p_rows(z, part, far), zf_send.at[part], zf_recv.at[z], (k, part))

    @pl.when(me == 0)
    def _():
        for d in range(1, size):
            src = flipped(k, d)
            for part in range(parts):
                remote(
                    tp_ref.at[src, part], t_send.at[d], t_recv.at[d, part], (win, me)
                ).wait_recv()
            for e in range(1, parts):
                from_lead(d, e).start()
            keep(d)

        def make_rows(index):
            rows = jnp.concatenate(
                [
                    t_ref[0, pl.ds(pl.multiple_of((part * size + index) * block, block), block), :]
                    for part in range(parts)
                ],
                axis=0,
            )
            for t in range(1, size):
                rows = dot3(split2(rows), (th_ref[t], tl_ref[t]))
            for part in range(parts):
                p_ref[z, part, pl.ds(pl.multiple_of(index * block, block), block), :] = rows[
                    part * block : (part + 1) * block
                ]

        pl.when(z > 0)(lambda: make_rows(k))
        for d in reversed(range(1, groups)):
            @pl.when(z >= d)
            def _():
                for part in range(parts):
                    to_group(d, part).start()

        @pl.when(jnp.logical_and(z > 0, z < groups - 1))
        def _():
            make_rows(far)
            for part in range(parts):
                to_first(part).start()

    @pl.when(me > 0)
    def _():
        for d in range(1, size):
            remote(tp_ref.at[flipped(k, d)], t_send.at[d], tf_recv.at[d], (win, me)).wait_recv()
            keep(d)

    for t in range(1, size):
        @pl.when(t > k)
        def _():
            v_ref[...] = dot3(split2(v_ref[...]), (th_ref[t], tl_ref[t]))

    def to_peer(d, e):
        return remote(p_rows(z + d, me, k), g_send.at[d, e], g_recv.at[d, e], peer(e))

    def to_sibling(d, e):
        return remote(p_ref.at[z + d, me], gf_send.at[d, e], gf_recv.at[d, me], sibling(e))

    def far_peer(d, act):
        if d == groups - 1:
            act()
        else:
            pl.when(z > 0)(act)

    def spread(d):
        remote(p_rows(z + d, me, k), z_send.at[d, 0], z_recv.at[d], (win, me)).wait_recv()
        far_peer(d, lambda: to_peer(d, size - 1).start())
        for e in range(1, size - 1):
            to_peer(d, e).start()

    def from_peer(d, e):
        remote(
            p_rows(z + d, me, flipped(k, e)), g_send.at[d, e], g_recv.at[d, e], peer(e)
        ).wait_recv()

    def share(d):
        for e in range(1, size - 1):
            from_peer(d, e)
        far_peer(d, lambda: from_peer(d, size - 1))
        if d < groups - 1:
            @pl.when(z == 0)
            def _():
                remote(
                    p_rows(d, me, far), zf_send.at[0], zf_recv.at[d], (win, me)
                ).wait_recv()
        for e in range(1, parts):
            to_sibling(d, e).start()

    def finish(d):
        for e in range(1, parts):
            part = lax.rem(me + parts - e, parts)
            remote(
                p_ref.at[z + d, part], gf_send.at[d, e], gf_recv.at[d, part], sibling(e)
            ).wait_recv()
        product = jnp.concatenate([p_ref[z + d, part] for part in range(parts)], axis=0)
        v_ref[...] = dot3(split2(v_ref[...]), split2(product))

    for step in range(1, groups + 2):
        for late, stage in enumerate((spread, share, finish)):
            if 1 <= step - late < groups:
                pl.when(z + step - late < groups)(functools.partial(stage, step - late))

    out_ref[0] = v_ref[...]

    for copy in sends:
        copy.wait_send()

    @pl.when(me == 0)
    def _():
        for d in range(1, size):
            for e in range(1, parts):
                from_lead(d, e).wait_send()
        for d in range(1, groups):
            @pl.when(z >= d)
            def _():
                for part in range(parts):
                    to_group(d, part).wait_send()

        @pl.when(jnp.logical_and(z > 0, z < groups - 1))
        def _():
            for part in range(parts):
                to_first(part).wait_send()

    for d in range(1, groups):
        @pl.when(z + d < groups)
        def _():
            for e in range(1, size - 1):
                to_peer(d, e).wait_send()
            far_peer(d, lambda: to_peer(d, size - 1).wait_send())
            for e in range(1, parts):
                to_sibling(d, e).wait_send()


def group_size(windows, parts, members):
    size = 1
    while size * size * 4 <= windows and windows % (size * 2) == 0 and members % (16 * size * parts) == 0:
        size *= 2
    return size


def solution(mesh):
    windows, parts = mesh.shape["win"], mesh.shape["state"]

    def shards(anomalies, mean_state, obs_rows, obs_precision):
        rows, members = anomalies.shape[1:]
        obs = obs_rows.shape[1]
        size = group_size(windows, parts, members)
        groups = windows // size
        dma = pltpu.SemaphoreType.DMA
        vmem = pl.BlockSpec(memory_space=pltpu.VMEM)
        return pl.pallas_call(
            functools.partial(kernel, groups, size, parts),
            out_shape=pltpu.VMEM(anomalies.shape, F32),
            in_specs=[pl.BlockSpec(memory_space=pltpu.HBM)] * 4,
            out_specs=vmem,
            scratch_shapes=[
                pltpu.VMEM((rows, members), F32),
                pltpu.VMEM((1, rows), F32),
                pltpu.VMEM((1, obs), jnp.int32),
                pltpu.VMEM((1, obs), F32),
                dma((4,)),
                pltpu.VMEM((parts, obs, members), F32),
                pltpu.VMEM((size, parts, members // (2 * parts) + 8, members), F32),
                pltpu.VMEM((size, members, members), F32),
                pltpu.VMEM((size, members, members), BF16),
                pltpu.VMEM((size, members, members), BF16),
                pltpu.VMEM((groups, parts, members // parts, members), F32),
                pltpu.VMEM((rows, members), F32),
                dma((parts,)), dma((parts,)),
                dma((size,)), dma((size, parts)),
                dma((size, parts)), dma((size,)),
                dma((groups, parts)), dma((groups,)), dma((parts,)), dma((groups,)),
                dma((groups, size)), dma((groups, size)),
                dma((groups, parts)), dma((groups, parts)),
            ],
            compiler_params=pltpu.CompilerParams(
                collective_id=0, has_side_effects=True, vmem_limit_bytes=56 * 1024 * 1024
            ),
        )(anomalies, mean_state, obs_rows, obs_precision)

    placed = (P("win", "state", None), P("win", "state"), P("win", "state"), P("win", "state"))
    return jax.shard_map(
        shards, mesh=mesh, in_specs=placed, out_specs=P("win", "state", None), check_vma=False
    )
```

```python
import functools

import jax
import jax.numpy as jnp
from jax import lax
from jax.experimental import pallas as pl
from jax.experimental.pallas import tpu as pltpu
from jax.sharding import PartitionSpec as P

NS_STEPS = 3
MESH = pl.DeviceIdType.MESH
F32 = jnp.float32
BF16 = jnp.bfloat16


def split2(x):
    hi = x.astype(BF16)
    return hi, (x - hi.astype(F32)).astype(BF16)


def mm(a, b):
    return jnp.dot(a, b, preferred_element_type=F32)


def dot3(a, b):
    (ah, al), (bh, bl) = a, b
    right = jnp.concatenate([bh, bl, bh], axis=0)
    half = ah.shape[0] // 2
    if half % 128:
        return mm(jnp.concatenate([ah, ah, al], axis=1), right)
    return jnp.concatenate(
        [
            mm(jnp.concatenate([h, h, l], axis=1), right)
            for h, l in ((ah[:half], al[:half]), (ah[half:], al[half:]))
        ],
        axis=0,
    )


def column(row, count):
    return jnp.transpose(jnp.broadcast_to(row, (8, count)))[:, :1]


def observed(x_ref, mean_ref, rows_ref, prec_ref):
    rows, members = x_ref.shape
    obs = rows_ref.shape[1]
    shifted = x_ref[...] + column(mean_ref[...], rows)
    wanted = column(rows_ref[...], obs)
    selector = (lax.broadcasted_iota(jnp.int32, (obs, rows), 1) == wanted).astype(BF16)
    hi = shifted.astype(BF16)
    rest = shifted - hi.astype(F32)
    mid = rest.astype(BF16)
    low = (rest - mid.astype(F32)).astype(BF16)
    predicted = jnp.tanh(mm(selector, hi) + mm(selector, mid) + mm(selector, low))
    centred = predicted - jnp.mean(predicted, axis=1, keepdims=True)
    return centred * jnp.sqrt(column(prec_ref[...], obs))


def gram_of(centred):
    left, right = split2(jnp.transpose(centred)), split2(centred)
    return dot3(left, right)


def inverse_root(gram):
    members = gram.shape[0]
    diagonal = lax.broadcasted_iota(jnp.int32, gram.shape, 0) == lax.broadcasted_iota(
        jnp.int32, gram.shape, 1
    )
    unit = diagonal.astype(F32)
    system = unit + gram
    root = system * (1.0 / jnp.sqrt(jnp.sum(system * system)))
    factor = 1.5 * unit - 0.5 * root
    inverse = split2(factor)
    root = split2(dot3(split2(root), inverse))
    full = None
    for step in range(1, NS_STEPS):
        factor = split2(1.5 * unit - 0.5 * dot3(inverse, root))
        if step + 1 < NS_STEPS:
            root = split2(dot3(root, factor))
        full = dot3(factor, inverse)
        inverse = split2(full)
    return full * (members / jnp.sum(jnp.where(diagonal, full, 0.0)))


def flipped(index, bits):
    result, bit = index, 1
    while bit <= bits:
        if bits & bit:
            result = result + bit * (1 - 2 * lax.rem(index // bit, 2))
        bit *= 2
    return result


def positions(half):
    return (
        lax.broadcasted_iota(jnp.int32, (half, half), 0),
        lax.broadcasted_iota(jnp.int32, (half, half), 1),
    )


def pack(matrix, ref, slot):
    half, parts, share = matrix.shape[0] // 2, ref.shape[1], ref.shape[2] - 8
    r, c = positions(half)
    upper, lower = matrix[:half, :half], matrix[half:, half:]
    both = jnp.where(r <= c, upper, lower)
    diagonal = jnp.sum(jnp.where(r == c, lower, 0.0), axis=0, keepdims=True)
    tail = jnp.broadcast_to(jnp.concatenate([diagonal, diagonal], axis=1), (8, 2 * half))
    for part in range(parts):
        rows = slice(part * share, (part + 1) * share)
        ref[slot, part, :share, :half] = both[rows]
        ref[slot, part, :share, half:] = matrix[rows, half:]
        ref[slot, part, share:, :] = tail


def unpacked(ref, slot):
    parts, share, half = ref.shape[1], ref.shape[2] - 8, ref.shape[3] // 2
    r, c = positions(half)
    rows = jnp.concatenate([ref[slot, part, :share, :] for part in range(parts)], axis=0)
    both, right = rows[:, :half], rows[:, half:]
    turned = jnp.transpose(both)
    diagonal = ref[slot, 0, share : share + 1, :half]
    upper = jnp.where(r <= c, both, turned)
    lower = jnp.where(r > c, both, jnp.where(r == c, diagonal, turned))
    return jnp.concatenate(
        [
            jnp.concatenate([upper, right], axis=1),
            jnp.concatenate([jnp.transpose(right), lower], axis=1),
        ],
        axis=0,
    )


def kernel(
    groups, size, parts, x_hbm, mean_hbm, rows_hbm, prec_hbm, out_ref,
    x_ref, mean_ref, rows_ref, prec_ref, in_sem, c_ref, tp_ref, t_ref, th_ref, tl_ref, p_ref, v_ref,
    c_send, c_recv, t_send, t_recv, tf_send, tf_recv,
    z_send, z_recv, zf_send, zf_recv, g_send, g_recv, gf_send, gf_recv,
):
    win, me = lax.axis_index("win"), lax.axis_index("state")
    z, k = win // size, lax.rem(win, size)
    fetches = [
        pltpu.make_async_copy(src, dst, in_sem.at[i])
        for i, (src, dst) in enumerate(
            [(mean_hbm, mean_ref), (rows_hbm, rows_ref), (prec_hbm, prec_ref), (x_hbm.at[0], x_ref)]
        )
    ]
    for fetch in fetches:
        fetch.start()
    members = x_ref.shape[1]
    block = members // (parts * size)

    def remote(ref, send, recv, device):
        return pltpu.make_async_remote_copy(
            src_ref=ref, dst_ref=ref, send_sem=send, recv_sem=recv,
            device_id=device, device_id_type=MESH,
        )

    def sibling(d):
        return win, lax.rem(me + d, parts)

    def peer(d):
        return z * size + flipped(k, d), me

    barrier = pltpu.get_barrier_semaphore()
    for e in range(1, parts):
        pl.semaphore_signal(barrier, inc=1, device_id=sibling(e), device_id_type=MESH)
    for e in range(parts):
        part = lax.rem(me + e, parts)
        for d in range(1, size):
            device = (z * size + flipped(k, d), part)
            pl.semaphore_signal(barrier, inc=1, device_id=device, device_id_type=MESH)
        for d in range(1, groups):
            device = (lax.rem(z + d, groups) * size + k, part)
            pl.semaphore_signal(barrier, inc=1, device_id=device, device_id_type=MESH)

    for fetch in fetches:
        fetch.wait()
    centred = observed(x_ref, mean_ref, rows_ref, prec_ref)
    c_ref[me] = centred
    pl.semaphore_wait(barrier, parts - 1 + parts * (size + groups - 2))

    sends = []
    for d in range(1, parts):
        copy = remote(c_ref.at[me], c_send.at[d], c_recv.at[me], sibling(d))
        copy.start()
        sends.append(copy)
    gram = gram_of(centred)
    for d in range(1, parts):
        src = lax.rem(me + parts - d, parts)
        remote(c_ref.at[src], c_send.at[d], c_recv.at[src], sibling(d)).wait_recv()
        gram = gram + gram_of(c_ref[src])
    transform = inverse_root(gram * (1.0 / (members - 1)))
    pack(transform, tp_ref, k)

    def to_lead(d, part):
        return remote(
            tp_ref.at[k, part], t_send.at[d], t_recv.at[d, part], (z * size + flipped(k, d), 0)
        )

    def from_lead(d, e):
        return remote(
            tp_ref.at[flipped(k, d)], tf_send.at[d, e], tf_recv.at[d], (win, e)
        )

    def keep(d):
        src = flipped(k, d)
        received = unpacked(tp_ref, src)
        t_ref[src] = received
        th_ref[src], tl_ref[src] = split2(received)

    for d in range(1, size):
        copy = to_lead(d, me)
        copy.start()
        sends.append(copy)
    own = split2(transform)
    t_ref[k], th_ref[k], tl_ref[k] = transform, own[0], own[1]
    v_ref[...] = dot3(split2(x_ref[...]), own)

    def p_rows(group, part, index):
        return p_ref.at[group, part, pl.ds(pl.multiple_of(index * block, block), block), :]

    def to_group(d, part):
        return remote(
            p_rows(z, part, k), z_send.at[d, part], z_recv.at[d], ((z - d) * size + k, part)
        )

    far = flipped(k, size - 1)

    def to_first(part):
        return remote(p_rows(z, part, far), zf_send.at[part], zf_recv.at[z], (k, part))

    @pl.when(me == 0)
    def _():
        for d in range(1, size):
            src = flipped(k, d)
            for part in range(parts):
                remote(
                    tp_ref.at[src, part], t_send.at[d], t_recv.at[d, part], (win, me)
                ).wait_recv()
            for e in range(1, parts):
                from_lead(d, e).start()
            keep(d)

        def make_rows(index):
            rows = jnp.concatenate(
                [
                    t_ref[0, pl.ds(pl.multiple_of((part * size + index) * block, block), block), :]
                    for part in range(parts)
                ],
                axis=0,
            )
            for t in range(1, size):
                rows = dot3(split2(rows), (th_ref[t], tl_ref[t]))
            for part in range(parts):
                p_ref[z, part, pl.ds(pl.multiple_of(index * block, block), block), :] = rows[
                    part * block : (part + 1) * block
                ]

        pl.when(z > 0)(lambda: make_rows(k))
        for d in reversed(range(1, groups)):
            @pl.when(z >= d)
            def _():
                for part in range(parts):
                    to_group(d, part).start()

        @pl.when(jnp.logical_and(z > 0, z < groups - 1))
        def _():
            make_rows(far)
            for part in range(parts):
                to_first(part).start()

    @pl.when(me > 0)
    def _():
        for d in range(1, size):
            remote(tp_ref.at[flipped(k, d)], t_send.at[d], tf_recv.at[d], (win, me)).wait_recv()
            keep(d)

    for t in range(1, size):
        @pl.when(t > k)
        def _():
            v_ref[...] = dot3(split2(v_ref[...]), (th_ref[t], tl_ref[t]))

    def to_peer(d, e):
        return remote(p_rows(z + d, me, k), g_send.at[d, e], g_recv.at[d, e], peer(e))

    def to_sibling(d, e):
        return remote(p_ref.at[z + d, me], gf_send.at[d, e], gf_recv.at[d, me], sibling(e))

    def far_peer(d, act):
        if d == groups - 1:
            act()
        else:
            pl.when(z > 0)(act)

    def spread(d):
        remote(p_rows(z + d, me, k), z_send.at[d, 0], z_recv.at[d], (win, me)).wait_recv()
        far_peer(d, lambda: to_peer(d, size - 1).start())
        for e in range(1, size - 1):
            to_peer(d, e).start()

    def from_peer(d, e):
        remote(
            p_rows(z + d, me, flipped(k, e)), g_send.at[d, e], g_recv.at[d, e], peer(e)
        ).wait_recv()

    def share(d):
        for e in range(1, size - 1):
            from_peer(d, e)
        far_peer(d, lambda: from_peer(d, size - 1))
        if d < groups - 1:
            @pl.when(z == 0)
            def _():
                remote(
                    p_rows(d, me, far), zf_send.at[0], zf_recv.at[d], (win, me)
                ).wait_recv()
        for e in range(1, parts):
            to_sibling(d, e).start()

    def finish(d):
        for e in range(1, parts):
            part = lax.rem(me + parts - e, parts)
            remote(
                p_ref.at[z + d, part], gf_send.at[d, e], gf_recv.at[d, part], sibling(e)
            ).wait_recv()
        product = jnp.concatenate([p_ref[z + d, part] for part in range(parts)], axis=0)
        v_ref[...] = dot3(split2(v_ref[...]), split2(product))

    for step in range(1, groups + 2):
        for late, stage in enumerate((spread, share, finish)):
            if 1 <= step - late < groups:
                pl.when(z + step - late < groups)(functools.partial(stage, step - late))

    out_ref[0] = v_ref[...]

    for copy in sends:
        copy.wait_send()

    @pl.when(me == 0)
    def _():
        for d in range(1, size):
            for e in range(1, parts):
                from_lead(d, e).wait_send()
        for d in range(1, groups):
            @pl.when(z >= d)
            def _():
                for part in range(parts):
                    to_group(d, part).wait_send()

        @pl.when(jnp.logical_and(z > 0, z < groups - 1))
        def _():
            for part in range(parts):
                to_first(part).wait_send()

    for d in range(1, groups):
        @pl.when(z + d < groups)
        def _():
            for e in range(1, size - 1):
                to_peer(d, e).wait_send()
            far_peer(d, lambda: to_peer(d, size - 1).wait_send())
            for e in range(1, parts):
                to_sibling(d, e).wait_send()


def group_size(windows, parts, members):
    size = 1
    while size * size * 4 <= windows and windows % (size * 2) == 0 and members % (16 * size * parts) == 0:
        size *= 2
    return size


def solution(mesh):
    windows, parts = mesh.shape["win"], mesh.shape["state"]

    def shards(anomalies, mean_state, obs_rows, obs_precision):
        rows, members = anomalies.shape[1:]
        obs = obs_rows.shape[1]
        size = group_size(windows, parts, members)
        groups = windows // size
        dma = pltpu.SemaphoreType.DMA
        vmem = pl.BlockSpec(memory_space=pltpu.VMEM)
        return pl.pallas_call(
            functools.partial(kernel, groups, size, parts),
            out_shape=pltpu.VMEM(anomalies.shape, F32),
            in_specs=[pl.BlockSpec(memory_space=pltpu.HBM)] * 4,
            out_specs=vmem,
            scratch_shapes=[
                pltpu.VMEM((rows, members), F32),
                pltpu.VMEM((1, rows), F32),
                pltpu.VMEM((1, obs), jnp.int32),
                pltpu.VMEM((1, obs), F32),
                dma((4,)),
                pltpu.VMEM((parts, obs, members), F32),
                pltpu.VMEM((size, parts, members // (2 * parts) + 8, members), F32),
                pltpu.VMEM((size, members, members), F32),
                pltpu.VMEM((size, members, members), BF16),
                pltpu.VMEM((size, members, members), BF16),
                pltpu.VMEM((groups, parts, members // parts, members), F32),
                pltpu.VMEM((rows, members), F32),
                dma((parts,)), dma((parts,)),
                dma((size,)), dma((size, parts)),
                dma((size, parts)), dma((size,)),
                dma((groups, parts)), dma((groups,)), dma((parts,)), dma((groups,)),
                dma((groups, size)), dma((groups, size)),
                dma((groups, parts)), dma((groups, parts)),
            ],
            compiler_params=pltpu.CompilerParams(
                collective_id=0, has_side_effects=True, vmem_limit_bytes=56 * 1024 * 1024
            ),
        )(anomalies, mean_state, obs_rows, obs_precision)

    placed = (P("win", "state", None), P("win", "state"), P("win", "state"), P("win", "state"))
    return jax.shard_map(
        shards, mesh=mesh, in_specs=placed, out_specs=P("win", "state", None), check_vma=False
    )
```

```python
import functools

import jax
import jax.numpy as jnp
from jax import lax
from jax.experimental import pallas as pl
from jax.experimental.pallas import tpu as pltpu
from jax.sharding import PartitionSpec as P

NS_STEPS = 3
MESH = pl.DeviceIdType.MESH
F32 = jnp.float32
BF16 = jnp.bfloat16


def split2(x):
    hi = x.astype(BF16)
    return hi, (x - hi.astype(F32)).astype(BF16)


def mm(a, b):
    return jnp.dot(a, b, preferred_element_type=F32)


def dot3(a, b):
    (ah, al), (bh, bl) = a, b
    return mm(jnp.concatenate([ah, ah, al], axis=1), jnp.concatenate([bh, bl, bh], axis=0))


def column(row, count):
    return jnp.transpose(jnp.broadcast_to(row, (8, count)))[:, :1]


def observed(x_ref, mean_ref, rows_ref, prec_ref):
    rows, members = x_ref.shape
    obs = rows_ref.shape[1]
    shifted = x_ref[...] + column(mean_ref[...], rows)
    wanted = column(rows_ref[...], obs)
    selector = (lax.broadcasted_iota(jnp.int32, (obs, rows), 1) == wanted).astype(BF16)
    hi = shifted.astype(BF16)
    rest = shifted - hi.astype(F32)
    mid = rest.astype(BF16)
    low = (rest - mid.astype(F32)).astype(BF16)
    predicted = jnp.tanh(mm(selector, hi) + mm(selector, mid) + mm(selector, low))
    centred = predicted - jnp.mean(predicted, axis=1, keepdims=True)
    return centred * jnp.sqrt(column(prec_ref[...], obs))


def gram_of(centred):
    left, right = split2(jnp.transpose(centred)), split2(centred)
    return dot3(left, right)


def inverse_root(gram):
    members = gram.shape[0]
    diagonal = lax.broadcasted_iota(jnp.int32, gram.shape, 0) == lax.broadcasted_iota(
        jnp.int32, gram.shape, 1
    )
    unit = diagonal.astype(F32)
    system = unit + gram
    root = system * (1.0 / jnp.sqrt(jnp.sum(system * system)))
    factor = 1.5 * unit - 0.5 * root
    inverse = split2(factor)
    root = split2(dot3(split2(root), inverse))
    full = None
    for step in range(1, NS_STEPS):
        factor = split2(1.5 * unit - 0.5 * dot3(inverse, root))
        if step + 1 < NS_STEPS:
            root = split2(dot3(root, factor))
        full = dot3(factor, inverse)
        inverse = split2(full)
    return full * (members / jnp.sum(jnp.where(diagonal, full, 0.0)))


def flipped(index, bits):
    result, bit = index, 1
    while bit <= bits:
        if bits & bit:
            result = result + bit * (1 - 2 * lax.rem(index // bit, 2))
        bit *= 2
    return result


def positions(half):
    return (
        lax.broadcasted_iota(jnp.int32, (half, half), 0),
        lax.broadcasted_iota(jnp.int32, (half, half), 1),
    )


def pack(matrix, ref, slot):
    half, parts, share = matrix.shape[0] // 2, ref.shape[1], ref.shape[2] - 8
    r, c = positions(half)
    upper, lower = matrix[:half, :half], matrix[half:, half:]
    both = jnp.where(r <= c, upper, lower)
    diagonal = jnp.sum(jnp.where(r == c, lower, 0.0), axis=0, keepdims=True)
    tail = jnp.broadcast_to(jnp.concatenate([diagonal, diagonal], axis=1), (8, 2 * half))
    for part in range(parts):
        rows = slice(part * share, (part + 1) * share)
        ref[slot, part, :share, :half] = both[rows]
        ref[slot, part, :share, half:] = matrix[rows, half:]
        ref[slot, part, share:, :] = tail


def unpacked(shares):
    share, half = shares[0].shape[0] - 8, shares[0].shape[1] // 2
    r, c = positions(half)
    rows = jnp.concatenate([part[:share] for part in shares], axis=0)
    both, right = rows[:, :half], rows[:, half:]
    turned = jnp.transpose(both)
    diagonal = shares[0][share : share + 1, :half]
    upper = jnp.where(r <= c, both, turned)
    lower = jnp.where(r > c, both, jnp.where(r == c, diagonal, turned))
    return jnp.concatenate(
        [
            jnp.concatenate([upper, right], axis=1),
            jnp.concatenate([jnp.transpose(right), lower], axis=1),
        ],
        axis=0,
    )


def kernel(
    groups, size, parts, x_hbm, mean_hbm, rows_hbm, prec_hbm, out_ref,
    x_ref, mean_ref, rows_ref, prec_ref, in_sem, c_ref, tp_ref, t_ref, th_ref, tl_ref, q_ref, p_ref, v_ref,
    c_send, c_recv, t_send, t_recv, tf_send, tf_recv,
    z_send, z_recv, g_send, g_recv, gf_send, gf_recv,
):
    win, me = lax.axis_index("win"), lax.axis_index("state")
    z, k = win // size, lax.rem(win, size)
    fetches = [
        pltpu.make_async_copy(src, dst, in_sem.at[i])
        for i, (src, dst) in enumerate(
            [(mean_hbm, mean_ref), (rows_hbm, rows_ref), (prec_hbm, prec_ref), (x_hbm.at[0], x_ref)]
        )
    ]
    for fetch in fetches:
        fetch.start()
    members = x_ref.shape[1]
    block = members // (parts * size)

    def remote(ref, send, recv, device):
        return pltpu.make_async_remote_copy(
            src_ref=ref, dst_ref=ref, send_sem=send, recv_sem=recv,
            device_id=device, device_id_type=MESH,
        )

    def sibling(d):
        return win, lax.rem(me + d, parts)

    def peer(d):
        return z * size + flipped(k, d), me

    barrier = pltpu.get_barrier_semaphore()
    for e in range(1, parts):
        pl.semaphore_signal(barrier, inc=1, device_id=sibling(e), device_id_type=MESH)
    for e in range(parts):
        part = lax.rem(me + e, parts)
        for d in range(1, size):
            device = (z * size + flipped(k, d), part)
            pl.semaphore_signal(barrier, inc=1, device_id=device, device_id_type=MESH)
        for d in range(1, groups):
            device = (lax.rem(z + d, groups) * size + k, part)
            pl.semaphore_signal(barrier, inc=1, device_id=device, device_id_type=MESH)

    for fetch in fetches:
        fetch.wait()
    centred = observed(x_ref, mean_ref, rows_ref, prec_ref)
    c_ref[me] = centred
    pl.semaphore_wait(barrier, parts - 1 + parts * (size + groups - 2))

    sends = []
    for d in range(1, parts):
        copy = remote(c_ref.at[me], c_send.at[d], c_recv.at[me], sibling(d))
        copy.start()
        sends.append(copy)
    gram = gram_of(centred)
    for d in range(1, parts):
        src = lax.rem(me + parts - d, parts)
        remote(c_ref.at[src], c_send.at[d], c_recv.at[src], sibling(d)).wait_recv()
        gram = gram + gram_of(c_ref[src])
    transform = inverse_root(gram * (1.0 / (members - 1)))
    pack(transform, tp_ref, k)

    def to_lead(d, part):
        return remote(
            tp_ref.at[k, part], t_send.at[d], t_recv.at[d, part], (z * size + flipped(k, d), 0)
        )

    def from_lead(d, e):
        return remote(
            tp_ref.at[flipped(k, d)], tf_send.at[d, e], tf_recv.at[d], (win, e)
        )

    def keep(d):
        src = flipped(k, d)
        received = unpacked([tp_ref[src, part] for part in range(parts)])
        t_ref[src] = received
        th_ref[src], tl_ref[src] = split2(received)

    def whole(d, part):
        return q_ref.at[part] if d == 1 else p_ref.at[z + d, part]

    def piece(d, index):
        return q_ref.at[me, index] if d == 1 else p_rows(z + d, me, index)

    def p_rows(group, part, index):
        return p_ref.at[group, part, pl.ds(pl.multiple_of(index * block, block), block), :]

    def to_previous():
        return pltpu.make_async_remote_copy(
            src_ref=tp_ref.at[k, me], dst_ref=q_ref.at[me, k], send_sem=z_send.at[1, 0],
            recv_sem=z_recv.at[1], device_id=((z - 1) * size + k, me), device_id_type=MESH,
        )

    def to_peer(d, e):
        return remote(piece(d, k), g_send.at[d, e], g_recv.at[d, e], peer(e))

    def to_sibling(d, e):
        return remote(whole(d, me), gf_send.at[d, e], gf_recv.at[d, me], sibling(e))

    def spread(d):
        remote(piece(d, k), z_send.at[d, 0], z_recv.at[d], (win, me)).wait_recv()
        for e in range(1, size):
            to_peer(d, e).start()

    def share(d):
        for e in range(1, size):
            remote(piece(d, flipped(k, e)), g_send.at[d, e], g_recv.at[d, e], peer(e)).wait_recv()
        for e in range(1, parts):
            to_sibling(d, e).start()

    def finish(d):
        for e in range(1, parts):
            part = lax.rem(me + parts - e, parts)
            remote(
                whole(d, part), gf_send.at[d, e], gf_recv.at[d, part], sibling(e)
            ).wait_recv()
        if d == 1:
            for t in range(size):
                later = unpacked([q_ref[part, t] for part in range(parts)])
                v_ref[...] = dot3(split2(v_ref[...]), split2(later))
        else:
            product = jnp.concatenate([p_ref[z + d, part] for part in range(parts)], axis=0)
            v_ref[...] = dot3(split2(v_ref[...]), split2(product))

    for d in range(1, size):
        copy = to_lead(d, me)
        copy.start()
        sends.append(copy)

    @pl.when(z > 0)
    def _():
        to_previous().start()

    own = split2(transform)
    t_ref[k], th_ref[k], tl_ref[k] = transform, own[0], own[1]
    v_ref[...] = dot3(split2(x_ref[...]), own)

    def to_group(d, part):
        return remote(
            p_rows(z, part, k), z_send.at[d, part], z_recv.at[d], ((z - d) * size + k, part)
        )

    @pl.when(me == 0)
    def _():
        for d in range(1, size):
            src = flipped(k, d)
            if d == size - 1:
                pl.when(z + 1 < groups)(functools.partial(spread, 1))
            for part in range(parts):
                remote(
                    tp_ref.at[src, part], t_send.at[d], t_recv.at[d, part], (win, me)
                ).wait_recv()
            for e in range(1, parts):
                from_lead(d, e).start()
            keep(d)

        @pl.when(z > 1)
        def _():
            rows = jnp.concatenate(
                [
                    t_ref[0, pl.ds(pl.multiple_of((part * size + k) * block, block), block), :]
                    for part in range(parts)
                ],
                axis=0,
            )
            for t in range(1, size):
                rows = dot3(split2(rows), (th_ref[t], tl_ref[t]))
            for part in range(parts):
                p_ref[z, part, pl.ds(pl.multiple_of(k * block, block), block), :] = rows[
                    part * block : (part + 1) * block
                ]

        for d in reversed(range(2, groups)):
            @pl.when(z >= d)
            def _():
                for part in range(parts):
                    to_group(d, part).start()

    @pl.when(me > 0)
    def _():
        for d in range(1, size):
            if d == size - 1:
                pl.when(z + 1 < groups)(functools.partial(spread, 1))
            remote(tp_ref.at[flipped(k, d)], t_send.at[d], tf_recv.at[d], (win, me)).wait_recv()
            keep(d)

    for t in range(1, size):
        @pl.when(t > k)
        def _():
            v_ref[...] = dot3(split2(v_ref[...]), (th_ref[t], tl_ref[t]))

    pl.when(z + 1 < groups)(functools.partial(share, 1))
    for d in range(2, groups):
        pl.when(z + d < groups)(functools.partial(spread, d))
    for d in range(1, groups):
        if d > 1:
            pl.when(z + d < groups)(functools.partial(share, d))
            pl.when(z + d - 1 < groups)(functools.partial(finish, d - 1))
        if d == groups - 1:
            pl.when(z + d < groups)(functools.partial(finish, d))

    out_ref[0] = v_ref[...]

    for copy in sends:
        copy.wait_send()

    @pl.when(me == 0)
    def _():
        for d in range(1, size):
            for e in range(1, parts):
                from_lead(d, e).wait_send()
        for d in range(2, groups):
            @pl.when(z >= d)
            def _():
                for part in range(parts):
                    to_group(d, part).wait_send()

    @pl.when(z > 0)
    def _():
        to_previous().wait_send()

    for d in range(1, groups):
        @pl.when(z + d < groups)
        def _():
            for e in range(1, size):
                to_peer(d, e).wait_send()
            for e in range(1, parts):
                to_sibling(d, e).wait_send()


def group_size(windows, parts, members):
    size = 1
    while size * size * 4 <= windows and windows % (size * 2) == 0 and members % (16 * size * parts) == 0:
        size *= 2
    return size


def solution(mesh):
    windows, parts = mesh.shape["win"], mesh.shape["state"]

    def shards(anomalies, mean_state, obs_rows, obs_precision):
        rows, members = anomalies.shape[1:]
        obs = obs_rows.shape[1]
        size = group_size(windows, parts, members)
        groups = windows // size
        dma = pltpu.SemaphoreType.DMA
        vmem = pl.BlockSpec(memory_space=pltpu.VMEM)
        return pl.pallas_call(
            functools.partial(kernel, groups, size, parts),
            out_shape=pltpu.VMEM(anomalies.shape, F32),
            in_specs=[pl.BlockSpec(memory_space=pltpu.HBM)] * 4,
            out_specs=vmem,
            scratch_shapes=[
                pltpu.VMEM((rows, members), F32),
                pltpu.VMEM((1, rows), F32),
                pltpu.VMEM((1, obs), jnp.int32),
                pltpu.VMEM((1, obs), F32),
                dma((4,)),
                pltpu.VMEM((parts, obs, members), F32),
                pltpu.VMEM((size, parts, members // (2 * parts) + 8, members), F32),
                pltpu.VMEM((size, members, members), F32),
                pltpu.VMEM((size, members, members), BF16),
                pltpu.VMEM((size, members, members), BF16),
                pltpu.VMEM((parts, size, members // (2 * parts) + 8, members), F32),
                pltpu.VMEM((groups, parts, members // parts, members), F32),
                pltpu.VMEM((rows, members), F32),
                dma((parts,)), dma((parts,)),
                dma((size,)), dma((size, parts)),
                dma((size, parts)), dma((size,)),
                dma((groups, parts)), dma((groups,)),
                dma((groups, size)), dma((groups, size)),
                dma((groups, parts)), dma((groups, parts)),
            ],
            compiler_params=pltpu.CompilerParams(
                collective_id=0, has_side_effects=True, vmem_limit_bytes=56 * 1024 * 1024
            ),
        )(anomalies, mean_state, obs_rows, obs_precision)

    placed = (P("win", "state", None), P("win", "state"), P("win", "state"), P("win", "state"))
    return jax.shard_map(
        shards, mesh=mesh, in_specs=placed, out_specs=P("win", "state", None), check_vma=False
    )
```

```python
import functools

import jax
import jax.numpy as jnp
from jax import lax
from jax.experimental import pallas as pl
from jax.experimental.pallas import tpu as pltpu
from jax.sharding import PartitionSpec as P

NS_STEPS = 3
MESH = pl.DeviceIdType.MESH
F32 = jnp.float32
BF16 = jnp.bfloat16


def split2(x):
    hi = x.astype(BF16)
    return hi, (x - hi.astype(F32)).astype(BF16)


def mm(a, b):
    return jnp.dot(a, b, preferred_element_type=F32)


def dot3(a, b):
    (ah, al), (bh, bl) = a, b
    return mm(jnp.concatenate([ah, ah, al], axis=1), jnp.concatenate([bh, bl, bh], axis=0))


def column(row, count):
    return jnp.transpose(jnp.broadcast_to(row, (8, count)))[:, :1]


def observed(x_ref, mean_ref, rows_ref, prec_ref):
    rows, members = x_ref.shape
    obs = rows_ref.shape[1]
    shifted = x_ref[...] + column(mean_ref[...], rows)
    wanted = column(rows_ref[...], obs)
    selector = (lax.broadcasted_iota(jnp.int32, (obs, rows), 1) == wanted).astype(BF16)
    hi = shifted.astype(BF16)
    rest = shifted - hi.astype(F32)
    mid = rest.astype(BF16)
    low = (rest - mid.astype(F32)).astype(BF16)
    predicted = jnp.tanh(mm(selector, hi) + mm(selector, mid) + mm(selector, low))
    centred = predicted - jnp.mean(predicted, axis=1, keepdims=True)
    return centred * jnp.sqrt(column(prec_ref[...], obs))


def gram_of(centred):
    left, right = split2(jnp.transpose(centred)), split2(centred)
    return dot3(left, right)


def inverse_root(gram):
    members = gram.shape[0]
    diagonal = lax.broadcasted_iota(jnp.int32, gram.shape, 0) == lax.broadcasted_iota(
        jnp.int32, gram.shape, 1
    )
    unit = diagonal.astype(F32)
    system = unit + gram
    root = system * (1.0 / jnp.sqrt(jnp.sum(system * system)))
    factor = 1.5 * unit - 0.5 * root
    inverse = split2(factor)
    root = split2(dot3(split2(root), inverse))
    full = None
    for step in range(1, NS_STEPS):
        factor = split2(1.5 * unit - 0.5 * dot3(inverse, root))
        if step + 1 < NS_STEPS:
            root = split2(dot3(root, factor))
        full = dot3(factor, inverse)
        inverse = split2(full)
    return full * (members / jnp.sum(jnp.where(diagonal, full, 0.0)))


def flipped(index, bits):
    result, bit = index, 1
    while bit <= bits:
        if bits & bit:
            result = result + bit * (1 - 2 * lax.rem(index // bit, 2))
        bit *= 2
    return result


def positions(half):
    return (
        lax.broadcasted_iota(jnp.int32, (half, half), 0),
        lax.broadcasted_iota(jnp.int32, (half, half), 1),
    )


def pack(matrix, ref, slot):
    half, parts, share = matrix.shape[0] // 2, ref.shape[1], ref.shape[2] - 8
    r, c = positions(half)
    upper, lower = matrix[:half, :half], matrix[half:, half:]
    both = jnp.where(r <= c, upper, lower)
    diagonal = jnp.sum(jnp.where(r == c, lower, 0.0), axis=0, keepdims=True)
    tail = jnp.broadcast_to(jnp.concatenate([diagonal, diagonal], axis=1), (8, 2 * half))
    for part in range(parts):
        rows = slice(part * share, (part + 1) * share)
        ref[slot, part, :share, :half] = both[rows]
        ref[slot, part, :share, half:] = matrix[rows, half:]
        ref[slot, part, share:, :] = tail


def unpacked(shares):
    share, half = shares[0].shape[0] - 8, shares[0].shape[1] // 2
    r, c = positions(half)
    rows = jnp.concatenate([part[:share] for part in shares], axis=0)
    both, right = rows[:, :half], rows[:, half:]
    turned = jnp.transpose(both)
    diagonal = shares[0][share : share + 1, :half]
    upper = jnp.where(r <= c, both, turned)
    lower = jnp.where(r > c, both, jnp.where(r == c, diagonal, turned))
    return jnp.concatenate(
        [
            jnp.concatenate([upper, right], axis=1),
            jnp.concatenate([jnp.transpose(right), lower], axis=1),
        ],
        axis=0,
    )


def kernel(
    groups, size, parts, x_hbm, mean_hbm, rows_hbm, prec_hbm, out_ref,
    x_ref, mean_ref, rows_ref, prec_ref, in_sem, c_ref, tp_ref, t_ref, th_ref, tl_ref, q_ref, p_ref, v_ref,
    c_send, c_recv, t_send, t_recv, tf_send, tf_recv,
    z_send, z_recv, g_send, g_recv, gf_send, gf_recv,
):
    win, me = lax.axis_index("win"), lax.axis_index("state")
    z, k = win // size, lax.rem(win, size)
    fetches = [
        pltpu.make_async_copy(src, dst, in_sem.at[i])
        for i, (src, dst) in enumerate(
            [(mean_hbm, mean_ref), (rows_hbm, rows_ref), (prec_hbm, prec_ref), (x_hbm.at[0], x_ref)]
        )
    ]
    for fetch in fetches:
        fetch.start()
    members = x_ref.shape[1]
    block = members // (parts * size)

    def remote(ref, send, recv, device):
        return pltpu.make_async_remote_copy(
            src_ref=ref, dst_ref=ref, send_sem=send, recv_sem=recv,
            device_id=device, device_id_type=MESH,
        )

    def sibling(d):
        return win, lax.rem(me + d, parts)

    def peer(d):
        return z * size + flipped(k, d), me

    barrier = pltpu.get_barrier_semaphore()
    for e in range(1, parts):
        pl.semaphore_signal(barrier, inc=1, device_id=sibling(e), device_id_type=MESH)
    for e in range(parts):
        part = lax.rem(me + e, parts)
        for d in range(1, size):
            device = (z * size + flipped(k, d), part)
            pl.semaphore_signal(barrier, inc=1, device_id=device, device_id_type=MESH)
        for d in range(1, groups):
            device = (lax.rem(z + d, groups) * size + k, part)
            pl.semaphore_signal(barrier, inc=1, device_id=device, device_id_type=MESH)

    for fetch in fetches:
        fetch.wait()
    centred = observed(x_ref, mean_ref, rows_ref, prec_ref)
    c_ref[me] = centred
    pl.semaphore_wait(barrier, parts - 1 + parts * (size + groups - 2))

    sends = []
    for d in range(1, parts):
        copy = remote(c_ref.at[me], c_send.at[d], c_recv.at[me], sibling(d))
        copy.start()
        sends.append(copy)
    gram = gram_of(centred)
    for d in range(1, parts):
        src = lax.rem(me + parts - d, parts)
        remote(c_ref.at[src], c_send.at[d], c_recv.at[src], sibling(d)).wait_recv()
        gram = gram + gram_of(c_ref[src])
    transform = inverse_root(gram * (1.0 / (members - 1)))
    pack(transform, tp_ref, k)

    share_rows = tp_ref.shape[2] - 8

    def packed(ref, first, second, part):
        return ref.at[first, second] if part == 0 else ref.at[first, second, pl.ds(0, share_rows), :]

    def by_part(act):
        pl.when(me == 0)(lambda: act(0))
        pl.when(me > 0)(lambda: act(1))

    def to_lead(d, kind):
        return remote(
            packed(tp_ref, k, me, kind), t_send.at[d], t_recv.at[d, me],
            (z * size + flipped(k, d), 0),
        )

    def from_lead(d, e):
        return remote(
            tp_ref.at[flipped(k, d)], tf_send.at[d, e], tf_recv.at[d], (win, e)
        )

    def keep(d):
        src = flipped(k, d)
        received = unpacked([tp_ref[src, part] for part in range(parts)])
        t_ref[src] = received
        th_ref[src], tl_ref[src] = split2(received)

    def whole(d, part):
        return q_ref.at[part] if d == 1 else p_ref.at[z + d, part]

    def piece(d, index, kind):
        return packed(q_ref, me, index, kind) if d == 1 else p_rows(z + d, me, index)

    def pieces(d, act):
        if d == 1:
            by_part(act)
        else:
            act(0)

    def p_rows(group, part, index):
        return p_ref.at[group, part, pl.ds(pl.multiple_of(index * block, block), block), :]

    def to_previous(kind):
        return pltpu.make_async_remote_copy(
            src_ref=packed(tp_ref, k, me, kind), dst_ref=packed(q_ref, me, k, kind), send_sem=z_send.at[1, 0],
            recv_sem=z_recv.at[1], device_id=((z - 1) * size + k, me), device_id_type=MESH,
        )

    def to_peer(d, e, kind):
        return remote(piece(d, k, kind), g_send.at[d, e], g_recv.at[d, e], peer(e))

    def to_sibling(d, e):
        return remote(whole(d, me), gf_send.at[d, e], gf_recv.at[d, me], sibling(e))

    def spread(d):
        def act(kind):
            remote(piece(d, k, kind), z_send.at[d, 0], z_recv.at[d], (win, me)).wait_recv()
            for e in range(1, size):
                to_peer(d, e, kind).start()

        pieces(d, act)

    def share(d):
        def act(kind):
            for e in range(1, size):
                remote(
                    piece(d, flipped(k, e), kind), g_send.at[d, e], g_recv.at[d, e], peer(e)
                ).wait_recv()

        pieces(d, act)
        for e in range(1, parts):
            to_sibling(d, e).start()

    def finish(d):
        for e in range(1, parts):
            part = lax.rem(me + parts - e, parts)
            remote(
                whole(d, part), gf_send.at[d, e], gf_recv.at[d, part], sibling(e)
            ).wait_recv()
        if d == 1:
            for t in range(size):
                later = unpacked([q_ref[part, t] for part in range(parts)])
                v_ref[...] = dot3(split2(v_ref[...]), split2(later))
        else:
            product = jnp.concatenate([p_ref[z + d, part] for part in range(parts)], axis=0)
            v_ref[...] = dot3(split2(v_ref[...]), split2(product))

    def send_own(kind):
        for d in range(1, size):
            to_lead(d, kind).start()
        pl.when(z > 0)(lambda: to_previous(kind).start())

    by_part(send_own)

    own = split2(transform)
    t_ref[k], th_ref[k], tl_ref[k] = transform, own[0], own[1]
    v_ref[...] = dot3(split2(x_ref[...]), own)

    def to_group(d, part):
        return remote(
            p_rows(z, part, k), z_send.at[d, part], z_recv.at[d], ((z - d) * size + k, part)
        )

    @pl.when(me == 0)
    def _():
        for d in range(1, size):
            src = flipped(k, d)
            if d == size - 1:
                pl.when(z + 1 < groups)(functools.partial(spread, 1))
            for part in range(parts):
                remote(
                    packed(tp_ref, src, part, part), t_send.at[d], t_recv.at[d, part], (win, me)
                ).wait_recv()
            for e in range(1, parts):
                from_lead(d, e).start()
            keep(d)

        @pl.when(z > 1)
        def _():
            rows = jnp.concatenate(
                [
                    t_ref[0, pl.ds(pl.multiple_of((part * size + k) * block, block), block), :]
                    for part in range(parts)
                ],
                axis=0,
            )
            for t in range(1, size):
                rows = dot3(split2(rows), (th_ref[t], tl_ref[t]))
            for part in range(parts):
                p_ref[z, part, pl.ds(pl.multiple_of(k * block, block), block), :] = rows[
                    part * block : (part + 1) * block
                ]

        for d in reversed(range(2, groups)):
            @pl.when(z >= d)
            def _():
                for part in range(parts):
                    to_group(d, part).start()

    @pl.when(me > 0)
    def _():
        for d in range(1, size):
            if d == size - 1:
                pl.when(z + 1 < groups)(functools.partial(spread, 1))
            remote(tp_ref.at[flipped(k, d)], t_send.at[d], tf_recv.at[d], (win, me)).wait_recv()
            keep(d)

    for t in range(1, size):
        @pl.when(t > k)
        def _():
            v_ref[...] = dot3(split2(v_ref[...]), (th_ref[t], tl_ref[t]))

    pl.when(z + 1 < groups)(functools.partial(share, 1))
    for d in range(2, groups):
        pl.when(z + d < groups)(functools.partial(spread, d))
    pl.when(z + 1 < groups)(functools.partial(finish, 1))
    for d in range(2, groups):
        pl.when(z + d < groups)(functools.partial(share, d))
        if d > 2:
            pl.when(z + d - 1 < groups)(functools.partial(finish, d - 1))
        if d == groups - 1:
            pl.when(z + d < groups)(functools.partial(finish, d))

    out_ref[0] = v_ref[...]

    for copy in sends:
        copy.wait_send()

    @pl.when(me == 0)
    def _():
        for d in range(1, size):
            for e in range(1, parts):
                from_lead(d, e).wait_send()
        for d in range(2, groups):
            @pl.when(z >= d)
            def _():
                for part in range(parts):
                    to_group(d, part).wait_send()

    def own_sent(kind):
        for d in range(1, size):
            to_lead(d, kind).wait_send()
        pl.when(z > 0)(lambda: to_previous(kind).wait_send())

    by_part(own_sent)

    for d in range(1, groups):
        @pl.when(z + d < groups)
        def _():
            def sent(kind):
                for e in range(1, size):
                    to_peer(d, e, kind).wait_send()

            pieces(d, sent)
            for e in range(1, parts):
                to_sibling(d, e).wait_send()


def group_size(windows, parts, members):
    size = 1
    while size * size * 4 <= windows and windows % (size * 2) == 0 and members % (16 * size * parts) == 0:
        size *= 2
    return size


def solution(mesh):
    windows, parts = mesh.shape["win"], mesh.shape["state"]

    def shards(anomalies, mean_state, obs_rows, obs_precision):
        rows, members = anomalies.shape[1:]
        obs = obs_rows.shape[1]
        size = group_size(windows, parts, members)
        groups = windows // size
        dma = pltpu.SemaphoreType.DMA
        vmem = pl.BlockSpec(memory_space=pltpu.VMEM)
        return pl.pallas_call(
            functools.partial(kernel, groups, size, parts),
            out_shape=pltpu.VMEM(anomalies.shape, F32),
            in_specs=[pl.BlockSpec(memory_space=pltpu.HBM)] * 4,
            out_specs=vmem,
            scratch_shapes=[
                pltpu.VMEM((rows, members), F32),
                pltpu.VMEM((1, rows), F32),
                pltpu.VMEM((1, obs), jnp.int32),
                pltpu.VMEM((1, obs), F32),
                dma((4,)),
                pltpu.VMEM((parts, obs, members), F32),
                pltpu.VMEM((size, parts, members // (2 * parts) + 8, members), F32),
                pltpu.VMEM((size, members, members), F32),
                pltpu.VMEM((size, members, members), BF16),
                pltpu.VMEM((size, members, members), BF16),
                pltpu.VMEM((parts, size, members // (2 * parts) + 8, members), F32),
                pltpu.VMEM((groups, parts, members // parts, members), F32),
                pltpu.VMEM((rows, members), F32),
                dma((parts,)), dma((parts,)),
                dma((size,)), dma((size, parts)),
                dma((size, parts)), dma((size,)),
                dma((groups, parts)), dma((groups,)),
                dma((groups, size)), dma((groups, size)),
                dma((groups, parts)), dma((groups, parts)),
            ],
            compiler_params=pltpu.CompilerParams(
                collective_id=0, has_side_effects=True, vmem_limit_bytes=56 * 1024 * 1024
            ),
        )(anomalies, mean_state, obs_rows, obs_precision)

    placed = (P("win", "state", None), P("win", "state"), P("win", "state"), P("win", "state"))
    return jax.shard_map(
        shards, mesh=mesh, in_specs=placed, out_specs=P("win", "state", None), check_vma=False
    )
```

```python
import functools

import jax
import jax.numpy as jnp
from jax import lax
from jax.experimental import pallas as pl
from jax.experimental.pallas import tpu as pltpu
from jax.sharding import PartitionSpec as P

NS_STEPS = 3
MESH = pl.DeviceIdType.MESH
F32 = jnp.float32
BF16 = jnp.bfloat16


def split2(x):
    hi = x.astype(BF16)
    return hi, (x - hi.astype(F32)).astype(BF16)


def mm(a, b):
    return jnp.dot(a, b, preferred_element_type=F32)


def dot3(a, b):
    (ah, al), (bh, bl) = a, b
    return mm(jnp.concatenate([ah, ah, al], axis=1), jnp.concatenate([bh, bl, bh], axis=0))


def column(row, count):
    return jnp.transpose(jnp.broadcast_to(row, (8, count)))[:, :1]


def observed(x_ref, mean_ref, rows_ref, prec_ref):
    rows, members = x_ref.shape
    obs = rows_ref.shape[1]
    shifted = x_ref[...] + column(mean_ref[...], rows)
    wanted = column(rows_ref[...], obs)
    selector = (lax.broadcasted_iota(jnp.int32, (obs, rows), 1) == wanted).astype(BF16)
    hi = shifted.astype(BF16)
    rest = shifted - hi.astype(F32)
    mid = rest.astype(BF16)
    low = (rest - mid.astype(F32)).astype(BF16)
    predicted = jnp.tanh(mm(selector, hi) + mm(selector, mid) + mm(selector, low))
    centred = predicted - jnp.mean(predicted, axis=1, keepdims=True)
    return centred * jnp.sqrt(column(prec_ref[...], obs))


def gram_of(centred):
    left, right = split2(jnp.transpose(centred)), split2(centred)
    return dot3(left, right)


def inverse_root(gram):
    members = gram.shape[0]
    diagonal = lax.broadcasted_iota(jnp.int32, gram.shape, 0) == lax.broadcasted_iota(
        jnp.int32, gram.shape, 1
    )
    unit = diagonal.astype(F32)
    system = unit + gram
    scale = 1.0 / jnp.sqrt(jnp.sum(system * system))
    parted = split2(system)
    square = dot3(parted, parted)
    full = 1.5 * unit - (0.5 * scale) * system
    root = split2((1.5 * scale) * system - (0.5 * scale * scale) * square)
    inverse = split2(full)
    trace = jnp.sum(jnp.where(diagonal, full, 0.0))
    for step in range(1, NS_STEPS):
        wide = 1.5 * unit - 0.5 * dot3(inverse, root)
        factor = split2(wide)
        if step + 1 < NS_STEPS:
            root = split2(dot3(root, factor))
        trace = jnp.sum(wide * full)
        full = dot3(factor, inverse)
        inverse = split2(full)
    return full * (members / trace)


def flipped(index, bits):
    result, bit = index, 1
    while bit <= bits:
        if bits & bit:
            result = result + bit * (1 - 2 * lax.rem(index // bit, 2))
        bit *= 2
    return result


def positions(half):
    return (
        lax.broadcasted_iota(jnp.int32, (half, half), 0),
        lax.broadcasted_iota(jnp.int32, (half, half), 1),
    )


def pack(matrix, ref, slot):
    half, parts, share = matrix.shape[0] // 2, ref.shape[1], ref.shape[2] - 8
    r, c = positions(half)
    upper, lower = matrix[:half, :half], matrix[half:, half:]
    both = jnp.where(r <= c, upper, lower)
    diagonal = jnp.sum(jnp.where(r == c, lower, 0.0), axis=0, keepdims=True)
    tail = jnp.broadcast_to(jnp.concatenate([diagonal, diagonal], axis=1), (8, 2 * half))
    for part in range(parts):
        rows = slice(part * share, (part + 1) * share)
        ref[slot, part, :share, :half] = both[rows]
        ref[slot, part, :share, half:] = matrix[rows, half:]
        ref[slot, part, share:, :] = tail


def unpacked(shares):
    share, half = shares[0].shape[0] - 8, shares[0].shape[1] // 2
    r, c = positions(half)
    rows = jnp.concatenate([part[:share] for part in shares], axis=0)
    both, right = rows[:, :half], rows[:, half:]
    turned = jnp.transpose(both)
    diagonal = shares[0][share : share + 1, :half]
    upper = jnp.where(r <= c, both, turned)
    lower = jnp.where(r > c, both, jnp.where(r == c, diagonal, turned))
    return jnp.concatenate(
        [
            jnp.concatenate([upper, right], axis=1),
            jnp.concatenate([jnp.transpose(right), lower], axis=1),
        ],
        axis=0,
    )


def kernel(
    groups, size, parts, x_hbm, mean_hbm, rows_hbm, prec_hbm, out_ref,
    x_ref, mean_ref, rows_ref, prec_ref, in_sem, c_ref, tp_ref, t_ref, th_ref, tl_ref, q_ref, p_ref, v_ref,
    c_send, c_recv, t_send, t_recv, tf_send, tf_recv,
    z_send, z_recv, zf_send, zf_recv, g_send, g_recv, gf_send, gf_recv,
):
    win, me = lax.axis_index("win"), lax.axis_index("state")
    z, k = win // size, lax.rem(win, size)
    fetches = [
        pltpu.make_async_copy(src, dst, in_sem.at[i])
        for i, (src, dst) in enumerate(
            [(mean_hbm, mean_ref), (rows_hbm, rows_ref), (prec_hbm, prec_ref), (x_hbm.at[0], x_ref)]
        )
    ]
    for fetch in fetches:
        fetch.start()
    members = x_ref.shape[1]
    block = members // (parts * size)

    def remote(ref, send, recv, device):
        return pltpu.make_async_remote_copy(
            src_ref=ref, dst_ref=ref, send_sem=send, recv_sem=recv,
            device_id=device, device_id_type=MESH,
        )

    def sibling(d):
        return win, lax.rem(me + d, parts)

    def peer(d):
        return z * size + flipped(k, d), me

    barrier = pltpu.get_barrier_semaphore()
    for e in range(1, parts):
        pl.semaphore_signal(barrier, inc=1, device_id=sibling(e), device_id_type=MESH)
    for e in range(parts):
        part = lax.rem(me + e, parts)
        for d in range(1, size):
            device = (z * size + flipped(k, d), part)
            pl.semaphore_signal(barrier, inc=1, device_id=device, device_id_type=MESH)
        for d in range(1, groups):
            device = (lax.rem(z + d, groups) * size + k, part)
            pl.semaphore_signal(barrier, inc=1, device_id=device, device_id_type=MESH)

    for fetch in fetches:
        fetch.wait()
    centred = observed(x_ref, mean_ref, rows_ref, prec_ref)
    c_ref[me] = centred
    pl.semaphore_wait(barrier, parts - 1 + parts * (size + groups - 2))

    sends = []
    for d in range(1, parts):
        copy = remote(c_ref.at[me], c_send.at[d], c_recv.at[me], sibling(d))
        copy.start()
        sends.append(copy)
    gram = gram_of(centred)
    for d in range(1, parts):
        src = lax.rem(me + parts - d, parts)
        remote(c_ref.at[src], c_send.at[d], c_recv.at[src], sibling(d)).wait_recv()
        gram = gram + gram_of(c_ref[src])
    transform = inverse_root(gram * (1.0 / (members - 1)))
    pack(transform, tp_ref, k)

    share_rows = tp_ref.shape[2] - 8

    def packed(ref, first, second, part):
        return ref.at[first, second] if part == 0 else ref.at[first, second, pl.ds(0, share_rows), :]

    def by_part(act):
        pl.when(me == 0)(lambda: act(0))
        pl.when(me > 0)(lambda: act(1))

    def to_lead(d, kind):
        return remote(
            packed(tp_ref, k, me, kind), t_send.at[d], t_recv.at[d, me],
            (z * size + flipped(k, d), 0),
        )

    def from_lead(d, e):
        return remote(
            tp_ref.at[flipped(k, d)], tf_send.at[d, e], tf_recv.at[d], (win, e)
        )

    def keep(d):
        src = flipped(k, d)
        received = unpacked([tp_ref[src, part] for part in range(parts)])
        t_ref[src] = received
        th_ref[src], tl_ref[src] = split2(received)

    def whole(d, part):
        return q_ref.at[part] if d == 1 else p_ref.at[z + d, part]

    def piece(d, index, kind):
        return packed(q_ref, me, index, kind) if d == 1 else p_rows(z + d, me, index)

    def pieces(d, act):
        if d == 1:
            by_part(act)
        else:
            act(0)

    def p_rows(group, part, index):
        return p_ref.at[group, part, pl.ds(pl.multiple_of(index * block, block), block), :]

    def to_previous(kind):
        return pltpu.make_async_remote_copy(
            src_ref=packed(tp_ref, k, me, kind), dst_ref=packed(q_ref, me, k, kind), send_sem=z_send.at[1, 0],
            recv_sem=z_recv.at[1], device_id=((z - 1) * size + k, me), device_id_type=MESH,
        )

    def to_peer(d, e, kind):
        return remote(piece(d, k, kind), g_send.at[d, e], g_recv.at[d, e], peer(e))

    def to_sibling(d, e):
        return remote(whole(d, me), gf_send.at[d, e], gf_recv.at[d, me], sibling(e))

    far = flipped(k, size - 1)

    def near(d):
        return range(1, size - 1 if d == groups - 1 else size)

    def spread(d):
        def act(kind):
            remote(piece(d, k, kind), z_send.at[d, 0], z_recv.at[d], (win, me)).wait_recv()
            for e in near(d):
                to_peer(d, e, kind).start()

        pieces(d, act)

    def share(d):
        def act(kind):
            for e in near(d):
                remote(
                    piece(d, flipped(k, e), kind), g_send.at[d, e], g_recv.at[d, e], peer(e)
                ).wait_recv()
            if d == groups - 1:
                remote(piece(d, far, kind), zf_send.at[0], zf_recv.at[0], (win, me)).wait_recv()

        pieces(d, act)
        for e in range(1, parts):
            to_sibling(d, e).start()

    def finish(d):
        for e in range(1, parts):
            part = lax.rem(me + parts - e, parts)
            remote(
                whole(d, part), gf_send.at[d, e], gf_recv.at[d, part], sibling(e)
            ).wait_recv()
        if d == 1:
            for t in range(size):
                later = unpacked([q_ref[part, t] for part in range(parts)])
                v_ref[...] = dot3(split2(v_ref[...]), split2(later))
        else:
            product = jnp.concatenate([p_ref[z + d, part] for part in range(parts)], axis=0)
            v_ref[...] = dot3(split2(v_ref[...]), split2(product))

    def send_own(kind):
        for d in range(1, size):
            to_lead(d, kind).start()
        pl.when(z > 0)(lambda: to_previous(kind).start())

    by_part(send_own)

    own = split2(transform)
    t_ref[k], th_ref[k], tl_ref[k] = transform, own[0], own[1]
    v_ref[...] = dot3(split2(x_ref[...]), own)

    def to_group(d, part):
        return remote(
            p_rows(z, part, k), z_send.at[d, part], z_recv.at[d], ((z - d) * size + k, part)
        )

    def to_first(part):
        return remote(p_rows(z, part, far), zf_send.at[part], zf_recv.at[0], (k, part))

    @pl.when(me == 0)
    def _():
        for d in range(1, size):
            src = flipped(k, d)
            if d == size - 1:
                pl.when(z + 1 < groups)(functools.partial(spread, 1))
            for part in range(parts):
                remote(
                    packed(tp_ref, src, part, part), t_send.at[d], t_recv.at[d, part], (win, me)
                ).wait_recv()
            for e in range(1, parts):
                from_lead(d, e).start()
            keep(d)

        def make_rows(index):
            rows = jnp.concatenate(
                [
                    t_ref[0, pl.ds(pl.multiple_of((part * size + index) * block, block), block), :]
                    for part in range(parts)
                ],
                axis=0,
            )
            for t in range(1, size):
                rows = dot3(split2(rows), (th_ref[t], tl_ref[t]))
            for part in range(parts):
                p_ref[z, part, pl.ds(pl.multiple_of(index * block, block), block), :] = rows[
                    part * block : (part + 1) * block
                ]

        pl.when(z > 1)(lambda: make_rows(k))
        for d in reversed(range(2, groups)):
            @pl.when(z >= d)
            def _():
                for part in range(parts):
                    to_group(d, part).start()

        @pl.when(z == groups - 1)
        def _():
            make_rows(far)
            for part in range(parts):
                to_first(part).start()

    @pl.when(me > 0)
    def _():
        for d in range(1, size):
            if d == size - 1:
                pl.when(z + 1 < groups)(functools.partial(spread, 1))
            remote(tp_ref.at[flipped(k, d)], t_send.at[d], tf_recv.at[d], (win, me)).wait_recv()
            keep(d)

    for t in range(1, size):
        @pl.when(t > k)
        def _():
            v_ref[...] = dot3(split2(v_ref[...]), (th_ref[t], tl_ref[t]))

    pl.when(z + 1 < groups)(functools.partial(share, 1))
    for d in range(2, groups):
        pl.when(z + d < groups)(functools.partial(spread, d))
    pl.when(z + 1 < groups)(functools.partial(finish, 1))
    for d in range(2, groups):
        pl.when(z + d < groups)(functools.partial(share, d))
        if d > 2:
            pl.when(z + d - 1 < groups)(functools.partial(finish, d - 1))
        if d == groups - 1:
            pl.when(z + d < groups)(functools.partial(finish, d))

    out_ref[0] = v_ref[...]

    for copy in sends:
        copy.wait_send()

    @pl.when(me == 0)
    def _():
        for d in range(1, size):
            for e in range(1, parts):
                from_lead(d, e).wait_send()
        for d in range(2, groups):
            @pl.when(z >= d)
            def _():
                for part in range(parts):
                    to_group(d, part).wait_send()

        @pl.when(z == groups - 1)
        def _():
            for part in range(parts):
                to_first(part).wait_send()

    def own_sent(kind):
        for d in range(1, size):
            to_lead(d, kind).wait_send()
        pl.when(z > 0)(lambda: to_previous(kind).wait_send())

    by_part(own_sent)

    for d in range(1, groups):
        @pl.when(z + d < groups)
        def _():
            def sent(kind):
                for e in near(d):
                    to_peer(d, e, kind).wait_send()

            pieces(d, sent)
            for e in range(1, parts):
                to_sibling(d, e).wait_send()


def group_size(windows, parts, members):
    size = 1
    while size * size * 4 <= windows and windows % (size * 2) == 0 and members % (16 * size * parts) == 0:
        size *= 2
    return size


def solution(mesh):
    windows, parts = mesh.shape["win"], mesh.shape["state"]

    def shards(anomalies, mean_state, obs_rows, obs_precision):
        rows, members = anomalies.shape[1:]
        obs = obs_rows.shape[1]
        size = group_size(windows, parts, members)
        groups = windows // size
        dma = pltpu.SemaphoreType.DMA
        vmem = pl.BlockSpec(memory_space=pltpu.VMEM)
        return pl.pallas_call(
            functools.partial(kernel, groups, size, parts),
            out_shape=pltpu.VMEM(anomalies.shape, F32),
            in_specs=[pl.BlockSpec(memory_space=pltpu.HBM)] * 4,
            out_specs=vmem,
            scratch_shapes=[
                pltpu.VMEM((rows, members), F32),
                pltpu.VMEM((1, rows), F32),
                pltpu.VMEM((1, obs), jnp.int32),
                pltpu.VMEM((1, obs), F32),
                dma((4,)),
                pltpu.VMEM((parts, obs, members), F32),
                pltpu.VMEM((size, parts, members // (2 * parts) + 8, members), F32),
                pltpu.VMEM((size, members, members), F32),
                pltpu.VMEM((size, members, members), BF16),
                pltpu.VMEM((size, members, members), BF16),
                pltpu.VMEM((parts, size, members // (2 * parts) + 8, members), F32),
                pltpu.VMEM((groups, parts, members // parts, members), F32),
                pltpu.VMEM((rows, members), F32),
                dma((parts,)), dma((parts,)),
                dma((size,)), dma((size, parts)),
                dma((size, parts)), dma((size,)),
                dma((groups, parts)), dma((groups,)), dma((parts,)), dma((1,)),
                dma((groups, size)), dma((groups, size)),
                dma((groups, parts)), dma((groups, parts)),
            ],
            compiler_params=pltpu.CompilerParams(
                collective_id=0, has_side_effects=True, vmem_limit_bytes=56 * 1024 * 1024
            ),
        )(anomalies, mean_state, obs_rows, obs_precision)

    placed = (P("win", "state", None), P("win", "state"), P("win", "state"), P("win", "state"))
    return jax.shard_map(
        shards, mesh=mesh, in_specs=placed, out_specs=P("win", "state", None), check_vma=False
    )
```

```python
import functools

import jax
import jax.numpy as jnp
from jax import lax
from jax.experimental import pallas as pl
from jax.experimental.pallas import tpu as pltpu
from jax.sharding import PartitionSpec as P

NS_STEPS = 3
MESH = pl.DeviceIdType.MESH
F32 = jnp.float32
BF16 = jnp.bfloat16


def split2(x):
    hi = x.astype(BF16)
    return hi, (x - hi.astype(F32)).astype(BF16)


def mm(a, b):
    return jnp.dot(a, b, preferred_element_type=F32)


def dot3(a, b):
    (ah, al), (bh, bl) = a, b
    return mm(jnp.concatenate([ah, ah, al], axis=1), jnp.concatenate([bh, bl, bh], axis=0))


def column(row, count):
    return jnp.transpose(jnp.broadcast_to(row, (8, count)))[:, :1]


def observed(x_ref, mean_ref, rows_ref, prec_ref):
    rows, members = x_ref.shape
    obs = rows_ref.shape[1]
    shifted = x_ref[...] + column(mean_ref[...], rows)
    wanted = column(rows_ref[...], obs)
    selector = (lax.broadcasted_iota(jnp.int32, (obs, rows), 1) == wanted).astype(BF16)
    hi = shifted.astype(BF16)
    rest = shifted - hi.astype(F32)
    mid = rest.astype(BF16)
    low = (rest - mid.astype(F32)).astype(BF16)
    predicted = jnp.tanh(mm(selector, hi) + mm(selector, mid) + mm(selector, low))
    centred = predicted - jnp.mean(predicted, axis=1, keepdims=True)
    return centred * jnp.sqrt(column(prec_ref[...], obs))


def gram_of(centred):
    left, right = split2(jnp.transpose(centred)), split2(centred)
    return dot3(left, right)


def inverse_root(gram):
    members = gram.shape[0]
    diagonal = lax.broadcasted_iota(jnp.int32, gram.shape, 0) == lax.broadcasted_iota(
        jnp.int32, gram.shape, 1
    )
    unit = diagonal.astype(F32)
    system = unit + gram
    scale = 1.0 / jnp.sqrt(jnp.sum(system * system))
    parted = split2(system)
    square = dot3(parted, parted)
    full = 1.5 * unit - (0.5 * scale) * system
    root = split2((1.5 * scale) * system - (0.5 * scale * scale) * square)
    inverse = split2(full)
    trace = jnp.sum(jnp.where(diagonal, full, 0.0))
    for step in range(1, NS_STEPS):
        wide = 1.5 * unit - 0.5 * dot3(inverse, root)
        factor = split2(wide)
        if step + 1 < NS_STEPS:
            root = split2(dot3(root, factor))
        trace = jnp.sum(wide * full)
        full = dot3(factor, inverse)
        inverse = split2(full)
    return full * (members / trace)


def flipped(index, bits):
    result, bit = index, 1
    while bit <= bits:
        if bits & bit:
            result = result + bit * (1 - 2 * lax.rem(index // bit, 2))
        bit *= 2
    return result


def positions(half):
    return (
        lax.broadcasted_iota(jnp.int32, (half, half), 0),
        lax.broadcasted_iota(jnp.int32, (half, half), 1),
    )


def pack(matrix, ref, slot):
    half, parts, share = matrix.shape[0] // 2, ref.shape[1], ref.shape[2] - 8
    r, c = positions(half)
    upper, lower = matrix[:half, :half], matrix[half:, half:]
    both = jnp.where(r <= c, upper, lower)
    diagonal = jnp.sum(jnp.where(r == c, lower, 0.0), axis=0, keepdims=True)
    tail = jnp.broadcast_to(jnp.concatenate([diagonal, diagonal], axis=1), (8, 2 * half))
    for part in range(parts):
        rows = slice(part * share, (part + 1) * share)
        ref[slot, part, :share, :half] = both[rows]
        ref[slot, part, :share, half:] = matrix[rows, half:]
        ref[slot, part, share:, :] = tail


def unpacked(shares):
    share, half = shares[0].shape[0] - 8, shares[0].shape[1] // 2
    r, c = positions(half)
    rows = jnp.concatenate([part[:share] for part in shares], axis=0)
    both, right = rows[:, :half], rows[:, half:]
    turned = jnp.transpose(both)
    diagonal = shares[0][share : share + 1, :half]
    upper = jnp.where(r <= c, both, turned)
    lower = jnp.where(r > c, both, jnp.where(r == c, diagonal, turned))
    return jnp.concatenate(
        [
            jnp.concatenate([upper, right], axis=1),
            jnp.concatenate([jnp.transpose(right), lower], axis=1),
        ],
        axis=0,
    )


def kernel(
    groups, size, parts, x_hbm, mean_hbm, rows_hbm, prec_hbm, out_ref,
    x_ref, mean_ref, rows_ref, prec_ref, in_sem, c_ref, tp_ref, t_ref, th_ref, tl_ref, q_ref, p_ref, v_ref,
    c_send, c_recv, t_send, t_recv, tf_send, tf_recv,
    z_send, z_recv, zf_send, zf_recv, g_send, g_recv, gf_send, gf_recv,
):
    win, me = lax.axis_index("win"), lax.axis_index("state")
    z, k = win // size, lax.rem(win, size)
    fetches = [
        pltpu.make_async_copy(src, dst, in_sem.at[i])
        for i, (src, dst) in enumerate(
            [(mean_hbm, mean_ref), (rows_hbm, rows_ref), (prec_hbm, prec_ref), (x_hbm.at[0], x_ref)]
        )
    ]
    for fetch in fetches:
        fetch.start()
    members = x_ref.shape[1]
    block = members // (parts * size)

    def remote(ref, send, recv, device):
        return pltpu.make_async_remote_copy(
            src_ref=ref, dst_ref=ref, send_sem=send, recv_sem=recv,
            device_id=device, device_id_type=MESH,
        )

    def sibling(d):
        return win, lax.rem(me + d, parts)

    def peer(d):
        return z * size + flipped(k, d), me

    barrier = pltpu.get_barrier_semaphore()
    for e in range(1, parts):
        pl.semaphore_signal(barrier, inc=1, device_id=sibling(e), device_id_type=MESH)
    for e in range(parts):
        part = lax.rem(me + e, parts)
        for d in range(1, size):
            device = (z * size + flipped(k, d), part)
            pl.semaphore_signal(barrier, inc=1, device_id=device, device_id_type=MESH)
        for d in range(1, groups):
            device = (lax.rem(z + d, groups) * size + k, part)
            pl.semaphore_signal(barrier, inc=1, device_id=device, device_id_type=MESH)

    for fetch in fetches:
        fetch.wait()
    centred = observed(x_ref, mean_ref, rows_ref, prec_ref)
    c_ref[me] = centred
    pl.semaphore_wait(barrier, parts - 1 + parts * (size + groups - 2))

    sends = []
    for d in range(1, parts):
        copy = remote(c_ref.at[me], c_send.at[d], c_recv.at[me], sibling(d))
        copy.start()
        sends.append(copy)
    gram = gram_of(centred)
    for d in range(1, parts):
        src = lax.rem(me + parts - d, parts)
        remote(c_ref.at[src], c_send.at[d], c_recv.at[src], sibling(d)).wait_recv()
        gram = gram + gram_of(c_ref[src])
    transform = inverse_root(gram * (1.0 / (members - 1)))
    pack(transform, tp_ref, k)

    share_rows = tp_ref.shape[2] - 8

    def packed(ref, first, second, part):
        return ref.at[first, second] if part == 0 else ref.at[first, second, pl.ds(0, share_rows), :]

    def by_part(act):
        pl.when(me == 0)(lambda: act(0))
        pl.when(me > 0)(lambda: act(1))

    def to_lead(d, kind):
        return remote(
            packed(tp_ref, k, me, kind), t_send.at[d], t_recv.at[d, me],
            (z * size + flipped(k, d), 0),
        )

    def from_lead(d, e):
        return remote(
            tp_ref.at[flipped(k, d)], tf_send.at[d, e], tf_recv.at[d], (win, e)
        )

    def keep(d):
        src = flipped(k, d)
        received = unpacked([tp_ref[src, part] for part in range(parts)])
        t_ref[src] = received
        th_ref[src], tl_ref[src] = split2(received)

    def whole(d, part):
        return q_ref.at[part] if d == 1 else p_ref.at[z + d, part]

    def piece(d, index, kind):
        return packed(q_ref, me, index, kind) if d == 1 else p_rows(z + d, me, index)

    def pieces(d, act):
        if d == 1:
            by_part(act)
        else:
            act(0)

    def p_rows(group, part, index):
        return p_ref.at[group, part, pl.ds(pl.multiple_of(index * block, block), block), :]

    def to_previous(kind):
        return pltpu.make_async_remote_copy(
            src_ref=packed(tp_ref, k, me, kind), dst_ref=packed(q_ref, me, k, kind), send_sem=z_send.at[1, 0],
            recv_sem=z_recv.at[1], device_id=((z - 1) * size + k, me), device_id_type=MESH,
        )

    def to_peer(d, e, kind):
        return remote(piece(d, k, kind), g_send.at[d, e], g_recv.at[d, e], peer(e))

    def to_sibling(d, e):
        return remote(whole(d, me), gf_send.at[d, e], gf_recv.at[d, me], sibling(e))

    far = flipped(k, size - 1)

    def near(d):
        return range(1, size - 1 if d == groups - 1 else size)

    def spread(d):
        def act(kind):
            remote(piece(d, k, kind), z_send.at[d, 0], z_recv.at[d], (win, me)).wait_recv()
            for e in reversed(near(d)):
                to_peer(d, e, kind).start()

        pieces(d, act)

    def share(d):
        def act(kind):
            for e in near(d):
                remote(
                    piece(d, flipped(k, e), kind), g_send.at[d, e], g_recv.at[d, e], peer(e)
                ).wait_recv()
            if d == groups - 1:
                remote(piece(d, far, kind), zf_send.at[0], zf_recv.at[0], (win, me)).wait_recv()

        pieces(d, act)
        for e in range(1, parts):
            to_sibling(d, e).start()

    def apply(first, last):
        for t in range(first, last):
            later = unpacked([q_ref[part, t] for part in range(parts)])
            v_ref[...] = dot3(split2(v_ref[...]), split2(later))

    def finish(d):
        for e in range(1, parts):
            part = lax.rem(me + parts - e, parts)
            remote(
                whole(d, part), gf_send.at[d, e], gf_recv.at[d, part], sibling(e)
            ).wait_recv()
        if d == 1:
            apply(0, size // 2)
        else:
            product = jnp.concatenate([p_ref[z + d, part] for part in range(parts)], axis=0)
            v_ref[...] = dot3(split2(v_ref[...]), split2(product))

    def send_own(kind):
        for d in reversed(range(1, size)):
            to_lead(d, kind).start()
        pl.when(z > 0)(lambda: to_previous(kind).start())

    by_part(send_own)

    own = split2(transform)
    t_ref[k], th_ref[k], tl_ref[k] = transform, own[0], own[1]
    v_ref[...] = dot3(split2(x_ref[...]), own)

    def to_group(d, part):
        return remote(
            p_rows(z, part, k), z_send.at[d, part], z_recv.at[d], ((z - d) * size + k, part)
        )

    def to_first(part):
        return remote(p_rows(z, part, far), zf_send.at[part], zf_recv.at[0], (k, part))

    @pl.when(me == 0)
    def _():
        for d in reversed(range(1, size)):
            src = flipped(k, d)
            if d == 1:
                pl.when(z + 1 < groups)(functools.partial(spread, 1))
            for part in range(parts):
                remote(
                    packed(tp_ref, src, part, part), t_send.at[d], t_recv.at[d, part], (win, me)
                ).wait_recv()
            for e in range(1, parts):
                from_lead(d, e).start()
            keep(d)

        def make_rows(index):
            rows = jnp.concatenate(
                [
                    t_ref[0, pl.ds(pl.multiple_of((part * size + index) * block, block), block), :]
                    for part in range(parts)
                ],
                axis=0,
            )
            for t in range(1, size):
                rows = dot3(split2(rows), (th_ref[t], tl_ref[t]))
            for part in range(parts):
                p_ref[z, part, pl.ds(pl.multiple_of(index * block, block), block), :] = rows[
                    part * block : (part + 1) * block
                ]

        pl.when(z > 1)(lambda: make_rows(k))
        for d in reversed(range(2, groups)):
            @pl.when(z >= d)
            def _():
                for part in range(parts):
                    to_group(d, part).start()

        @pl.when(z == groups - 1)
        def _():
            make_rows(far)
            for part in range(parts):
                to_first(part).start()

    @pl.when(me > 0)
    def _():
        for d in reversed(range(1, size)):
            if d == 1:
                pl.when(z + 1 < groups)(functools.partial(spread, 1))
            remote(tp_ref.at[flipped(k, d)], t_send.at[d], tf_recv.at[d], (win, me)).wait_recv()
            keep(d)

    for t in range(1, size):
        @pl.when(t > k)
        def _():
            v_ref[...] = dot3(split2(v_ref[...]), (th_ref[t], tl_ref[t]))

    pl.when(z + 1 < groups)(functools.partial(share, 1))
    for d in range(2, groups):
        pl.when(z + d < groups)(functools.partial(spread, d))
        if d == 2:
            pl.when(z + 1 < groups)(functools.partial(finish, 1))
    pl.when(z + 1 < groups)(lambda: apply(size // 2, size))
    for d in range(2, groups):
        pl.when(z + d < groups)(functools.partial(share, d))
        if d > 2:
            pl.when(z + d - 1 < groups)(functools.partial(finish, d - 1))
        if d == groups - 1:
            pl.when(z + d < groups)(functools.partial(finish, d))

    out_ref[0] = v_ref[...]

    for copy in sends:
        copy.wait_send()

    @pl.when(me == 0)
    def _():
        for d in range(1, size):
            for e in range(1, parts):
                from_lead(d, e).wait_send()
        for d in range(2, groups):
            @pl.when(z >= d)
            def _():
                for part in range(parts):
                    to_group(d, part).wait_send()

        @pl.when(z == groups - 1)
        def _():
            for part in range(parts):
                to_first(part).wait_send()

    def own_sent(kind):
        for d in range(1, size):
            to_lead(d, kind).wait_send()
        pl.when(z > 0)(lambda: to_previous(kind).wait_send())

    by_part(own_sent)

    for d in range(1, groups):
        @pl.when(z + d < groups)
        def _():
            def sent(kind):
                for e in near(d):
                    to_peer(d, e, kind).wait_send()

            pieces(d, sent)
            for e in range(1, parts):
                to_sibling(d, e).wait_send()


def group_size(windows, parts, members):
    size = 1
    while size * size * 4 <= windows and windows % (size * 2) == 0 and members % (16 * size * parts) == 0:
        size *= 2
    return size


def solution(mesh):
    windows, parts = mesh.shape["win"], mesh.shape["state"]

    def shards(anomalies, mean_state, obs_rows, obs_precision):
        rows, members = anomalies.shape[1:]
        obs = obs_rows.shape[1]
        size = group_size(windows, parts, members)
        groups = windows // size
        dma = pltpu.SemaphoreType.DMA
        vmem = pl.BlockSpec(memory_space=pltpu.VMEM)
        return pl.pallas_call(
            functools.partial(kernel, groups, size, parts),
            out_shape=pltpu.VMEM(anomalies.shape, F32),
            in_specs=[pl.BlockSpec(memory_space=pltpu.HBM)] * 4,
            out_specs=vmem,
            scratch_shapes=[
                pltpu.VMEM((rows, members), F32),
                pltpu.VMEM((1, rows), F32),
                pltpu.VMEM((1, obs), jnp.int32),
                pltpu.VMEM((1, obs), F32),
                dma((4,)),
                pltpu.VMEM((parts, obs, members), F32),
                pltpu.VMEM((size, parts, members // (2 * parts) + 8, members), F32),
                pltpu.VMEM((size, members, members), F32),
                pltpu.VMEM((size, members, members), BF16),
                pltpu.VMEM((size, members, members), BF16),
                pltpu.VMEM((parts, size, members // (2 * parts) + 8, members), F32),
                pltpu.VMEM((groups, parts, members // parts, members), F32),
                pltpu.VMEM((rows, members), F32),
                dma((parts,)), dma((parts,)),
                dma((size,)), dma((size, parts)),
                dma((size, parts)), dma((size,)),
                dma((groups, parts)), dma((groups,)), dma((parts,)), dma((1,)),
                dma((groups, size)), dma((groups, size)),
                dma((groups, parts)), dma((groups, parts)),
            ],
            compiler_params=pltpu.CompilerParams(
                collective_id=0, has_side_effects=True, vmem_limit_bytes=56 * 1024 * 1024
            ),
        )(anomalies, mean_state, obs_rows, obs_precision)

    placed = (P("win", "state", None), P("win", "state"), P("win", "state"), P("win", "state"))
    return jax.shard_map(
        shards, mesh=mesh, in_specs=placed, out_specs=P("win", "state", None), check_vma=False
    )
```

```python
import functools

import jax
import jax.numpy as jnp
from jax import lax
from jax.experimental import pallas as pl
from jax.experimental.pallas import tpu as pltpu
from jax.sharding import PartitionSpec as P

NS_STEPS = 3
MESH = pl.DeviceIdType.MESH
F32 = jnp.float32
BF16 = jnp.bfloat16


def split2(x):
    hi = x.astype(BF16)
    return hi, (x - hi.astype(F32)).astype(BF16)


def mm(a, b):
    return jnp.dot(a, b, preferred_element_type=F32)


def dot3(a, b):
    (ah, al), (bh, bl) = a, b
    return mm(jnp.concatenate([ah, ah, al], axis=1), jnp.concatenate([bh, bl, bh], axis=0))


def column(row, count):
    return jnp.transpose(jnp.broadcast_to(row, (8, count)))[:, :1]


def observed(x_ref, mean_ref, rows_ref, prec_ref):
    rows, members = x_ref.shape
    obs = rows_ref.shape[1]
    shifted = x_ref[...] + column(mean_ref[...], rows)
    wanted = column(rows_ref[...], obs)
    selector = (lax.broadcasted_iota(jnp.int32, (obs, rows), 1) == wanted).astype(BF16)
    hi = shifted.astype(BF16)
    rest = shifted - hi.astype(F32)
    mid = rest.astype(BF16)
    low = (rest - mid.astype(F32)).astype(BF16)
    predicted = jnp.tanh(mm(selector, hi) + mm(selector, mid) + mm(selector, low))
    centred = predicted - jnp.mean(predicted, axis=1, keepdims=True)
    return centred * jnp.sqrt(column(prec_ref[...], obs))


def gram_of(centred):
    left, right = split2(jnp.transpose(centred)), split2(centred)
    return dot3(left, right)


def inverse_root(gram):
    members = gram.shape[0]
    diagonal = lax.broadcasted_iota(jnp.int32, gram.shape, 0) == lax.broadcasted_iota(
        jnp.int32, gram.shape, 1
    )
    unit = diagonal.astype(F32)
    system = unit + gram
    scale = 1.0 / jnp.sqrt(jnp.sum(system * system))
    parted = split2(system)
    square = dot3(parted, parted)
    full = 1.5 * unit - (0.5 * scale) * system
    root = split2((1.5 * scale) * system - (0.5 * scale * scale) * square)
    inverse = split2(full)
    trace = jnp.sum(jnp.where(diagonal, full, 0.0))
    for step in range(1, NS_STEPS):
        wide = 1.5 * unit - 0.5 * dot3(inverse, root)
        factor = split2(wide)
        if step + 1 < NS_STEPS:
            root = split2(dot3(root, factor))
        trace = jnp.sum(wide * full)
        full = dot3(factor, inverse)
        inverse = split2(full)
    return full * (members / trace)


def flipped(index, bits):
    result, bit = index, 1
    while bit <= bits:
        if bits & bit:
            result = result + bit * (1 - 2 * lax.rem(index // bit, 2))
        bit *= 2
    return result


def positions(half):
    return (
        lax.broadcasted_iota(jnp.int32, (half, half), 0),
        lax.broadcasted_iota(jnp.int32, (half, half), 1),
    )


def pack(matrix, ref, slot):
    half, parts, share = matrix.shape[0] // 2, ref.shape[1], ref.shape[2] - 8
    r, c = positions(half)
    upper, lower = matrix[:half, :half], matrix[half:, half:]
    both = jnp.where(r <= c, upper, lower)
    diagonal = jnp.sum(jnp.where(r == c, lower, 0.0), axis=0, keepdims=True)
    tail = jnp.broadcast_to(jnp.concatenate([diagonal, diagonal], axis=1), (8, 2 * half))
    for part in range(parts):
        rows = slice(part * share, (part + 1) * share)
        ref[slot, part, :share, :half] = both[rows]
        ref[slot, part, :share, half:] = matrix[rows, half:]
        ref[slot, part, share:, :] = tail


def unpacked(shares):
    share, half = shares[0].shape[0] - 8, shares[0].shape[1] // 2
    r, c = positions(half)
    rows = jnp.concatenate([part[:share] for part in shares], axis=0)
    both, right = rows[:, :half], rows[:, half:]
    turned = jnp.transpose(both)
    diagonal = shares[0][share : share + 1, :half]
    upper = jnp.where(r <= c, both, turned)
    lower = jnp.where(r > c, both, jnp.where(r == c, diagonal, turned))
    return jnp.concatenate(
        [
            jnp.concatenate([upper, right], axis=1),
            jnp.concatenate([jnp.transpose(right), lower], axis=1),
        ],
        axis=0,
    )


def kernel(
    groups, size, parts, x_hbm, mean_hbm, rows_hbm, prec_hbm, out_ref,
    x_ref, mean_ref, rows_ref, prec_ref, in_sem, c_ref, tp_ref, t_ref, th_ref, tl_ref, q_ref, p_ref, v_ref,
    c_send, c_recv, t_send, t_recv, tf_send, tf_recv,
    z_send, z_recv, zf_send, zf_recv, g_send, g_recv, gf_send, gf_recv,
):
    win, me = lax.axis_index("win"), lax.axis_index("state")
    z, k = win // size, lax.rem(win, size)
    fetches = [
        pltpu.make_async_copy(src, dst, in_sem.at[i])
        for i, (src, dst) in enumerate(
            [(mean_hbm, mean_ref), (rows_hbm, rows_ref), (prec_hbm, prec_ref), (x_hbm.at[0], x_ref)]
        )
    ]
    for fetch in fetches:
        fetch.start()
    members = x_ref.shape[1]
    block = members // (parts * size)

    def remote(ref, send, recv, device):
        return pltpu.make_async_remote_copy(
            src_ref=ref, dst_ref=ref, send_sem=send, recv_sem=recv,
            device_id=device, device_id_type=MESH,
        )

    def sibling(d):
        return win, lax.rem(me + d, parts)

    def peer(d):
        return z * size + flipped(k, d), me

    barrier = pltpu.get_barrier_semaphore()
    for e in range(1, parts):
        pl.semaphore_signal(barrier, inc=1, device_id=sibling(e), device_id_type=MESH)
    for e in range(parts):
        part = lax.rem(me + e, parts)
        for d in range(1, size):
            device = (z * size + flipped(k, d), part)
            pl.semaphore_signal(barrier, inc=1, device_id=device, device_id_type=MESH)
        for d in range(1, groups):
            device = (lax.rem(z + d, groups) * size + k, part)
            pl.semaphore_signal(barrier, inc=1, device_id=device, device_id_type=MESH)

    for fetch in fetches:
        fetch.wait()
    centred = observed(x_ref, mean_ref, rows_ref, prec_ref)
    c_ref[me] = centred
    pl.semaphore_wait(barrier, parts - 1 + parts * (size + groups - 2))

    sends = []
    for d in range(1, parts):
        copy = remote(c_ref.at[me], c_send.at[d], c_recv.at[me], sibling(d))
        copy.start()
        sends.append(copy)
    gram = gram_of(centred)
    for d in range(1, parts):
        src = lax.rem(me + parts - d, parts)
        remote(c_ref.at[src], c_send.at[d], c_recv.at[src], sibling(d)).wait_recv()
        gram = gram + gram_of(c_ref[src])
    transform = inverse_root(gram * (1.0 / (members - 1)))
    pack(transform, tp_ref, k)

    share_rows = tp_ref.shape[2] - 8

    def packed(ref, first, second, part):
        return ref.at[first, second] if part == 0 else ref.at[first, second, pl.ds(0, share_rows), :]

    def by_part(act):
        pl.when(me == 0)(lambda: act(0))
        pl.when(me > 0)(lambda: act(1))

    def to_lead(d, kind):
        return remote(
            packed(tp_ref, k, me, kind), t_send.at[d], t_recv.at[d, me],
            (z * size + flipped(k, d), 0),
        )

    def from_lead(d, e):
        return remote(
            tp_ref.at[flipped(k, d)], tf_send.at[d, e], tf_recv.at[d], (win, e)
        )

    def keep(d):
        src = flipped(k, d)
        received = unpacked([tp_ref[src, part] for part in range(parts)])
        t_ref[src] = received
        th_ref[src], tl_ref[src] = split2(received)

    def whole(d, part):
        return q_ref.at[part] if d == 1 else p_ref.at[z + d, part]

    def piece(d, index, kind):
        return packed(q_ref, me, index, kind) if d == 1 else p_rows(z + d, me, index)

    def pieces(d, act):
        if d == 1:
            by_part(act)
        else:
            act(0)

    def p_rows(group, part, index):
        return p_ref.at[group, part, pl.ds(pl.multiple_of(index * block, block), block), :]

    def to_previous(kind):
        return pltpu.make_async_remote_copy(
            src_ref=packed(tp_ref, k, me, kind), dst_ref=packed(q_ref, me, k, kind), send_sem=z_send.at[1, 0],
            recv_sem=z_recv.at[1], device_id=((z - 1) * size + k, me), device_id_type=MESH,
        )

    def to_peer(d, e, kind):
        return remote(piece(d, k, kind), g_send.at[d, e], g_recv.at[d, e], peer(e))

    def to_sibling(d, e):
        return remote(whole(d, me), gf_send.at[d, e], gf_recv.at[d, me], sibling(e))

    far = flipped(k, size - 1)

    def near(d):
        return range(1, size - 1 if d == groups - 1 else size)

    def spread(d):
        def act(kind):
            remote(piece(d, k, kind), z_send.at[d, 0], z_recv.at[d], (win, me)).wait_recv()
            for e in reversed(near(d)):
                to_peer(d, e, kind).start()

        pieces(d, act)

    def share(d):
        def act(kind):
            for e in near(d):
                remote(
                    piece(d, flipped(k, e), kind), g_send.at[d, e], g_recv.at[d, e], peer(e)
                ).wait_recv()
            if d == groups - 1:
                remote(piece(d, far, kind), zf_send.at[0], zf_recv.at[0], (win, me)).wait_recv()

        pieces(d, act)
        for e in range(1, parts):
            to_sibling(d, e).start()

    def finish(d):
        for e in range(1, parts):
            part = lax.rem(me + parts - e, parts)
            remote(
                whole(d, part), gf_send.at[d, e], gf_recv.at[d, part], sibling(e)
            ).wait_recv()
        if d == 1:
            for t in range(size):
                later = unpacked([q_ref[part, t] for part in range(parts)])
                v_ref[...] = dot3(split2(v_ref[...]), split2(later))
        else:
            product = jnp.concatenate([p_ref[z + d, part] for part in range(parts)], axis=0)
            v_ref[...] = dot3(split2(v_ref[...]), split2(product))

    def send_own(kind):
        for d in reversed(range(1, size)):
            to_lead(d, kind).start()
        pl.when(z > 0)(lambda: to_previous(kind).start())

    by_part(send_own)

    own = split2(transform)
    t_ref[k], th_ref[k], tl_ref[k] = transform, own[0], own[1]
    v_ref[...] = dot3(split2(x_ref[...]), own)

    def to_group(d, part):
        return remote(
            p_rows(z, part, k), z_send.at[d, part], z_recv.at[d], ((z - d) * size + k, part)
        )

    def to_first(part):
        return remote(p_rows(z, part, far), zf_send.at[part], zf_recv.at[0], (k, part))

    @pl.when(me == 0)
    def _():
        for d in reversed(range(1, size)):
            src = flipped(k, d)
            if d == 1:
                pl.when(z + 1 < groups)(functools.partial(spread, 1))
            for part in range(parts):
                remote(
                    packed(tp_ref, src, part, part), t_send.at[d], t_recv.at[d, part], (win, me)
                ).wait_recv()
            for e in range(1, parts):
                from_lead(d, e).start()
            keep(d)

        def make_rows(index):
            rows = jnp.concatenate(
                [
                    t_ref[0, pl.ds(pl.multiple_of((part * size + index) * block, block), block), :]
                    for part in range(parts)
                ],
                axis=0,
            )
            for t in range(1, size):
                rows = dot3(split2(rows), (th_ref[t], tl_ref[t]))
            for part in range(parts):
                p_ref[z, part, pl.ds(pl.multiple_of(index * block, block), block), :] = rows[
                    part * block : (part + 1) * block
                ]

        pl.when(z > 1)(lambda: make_rows(k))
        for d in reversed(range(2, groups)):
            @pl.when(z >= d)
            def _():
                for part in range(parts):
                    to_group(d, part).start()

        @pl.when(z == groups - 1)
        def _():
            make_rows(far)
            for part in range(parts):
                to_first(part).start()

    @pl.when(me > 0)
    def _():
        for d in reversed(range(1, size)):
            if d == 1:
                pl.when(z + 1 < groups)(functools.partial(spread, 1))
            remote(tp_ref.at[flipped(k, d)], t_send.at[d], tf_recv.at[d], (win, me)).wait_recv()
            keep(d)

    for t in range(1, size):
        @pl.when(t > k)
        def _():
            v_ref[...] = dot3(split2(v_ref[...]), (th_ref[t], tl_ref[t]))

    pl.when(z + 1 < groups)(functools.partial(share, 1))
    for d in range(2, groups):
        pl.when(z + d < groups)(functools.partial(spread, d))
    pl.when(z + 1 < groups)(functools.partial(finish, 1))
    for d in range(2, groups):
        pl.when(z + d < groups)(functools.partial(share, d))
        if d > 2:
            pl.when(z + d - 1 < groups)(functools.partial(finish, d - 1))
        if d == groups - 1:
            pl.when(z + d < groups)(functools.partial(finish, d))

    out_ref[0] = v_ref[...]

    for copy in sends:
        copy.wait_send()

    @pl.when(me == 0)
    def _():
        for d in range(1, size):
            for e in range(1, parts):
                from_lead(d, e).wait_send()
        for d in range(2, groups):
            @pl.when(z >= d)
            def _():
                for part in range(parts):
                    to_group(d, part).wait_send()

        @pl.when(z == groups - 1)
        def _():
            for part in range(parts):
                to_first(part).wait_send()

    def own_sent(kind):
        for d in range(1, size):
            to_lead(d, kind).wait_send()
        pl.when(z > 0)(lambda: to_previous(kind).wait_send())

    by_part(own_sent)

    for d in range(1, groups):
        @pl.when(z + d < groups)
        def _():
            def sent(kind):
                for e in near(d):
                    to_peer(d, e, kind).wait_send()

            pieces(d, sent)
            for e in range(1, parts):
                to_sibling(d, e).wait_send()


def group_size(windows, parts, members):
    size = 1
    while size * size * 4 <= windows and windows % (size * 2) == 0 and members % (16 * size * parts) == 0:
        size *= 2
    return size


def solution(mesh):
    windows, parts = mesh.shape["win"], mesh.shape["state"]

    def shards(anomalies, mean_state, obs_rows, obs_precision):
        rows, members = anomalies.shape[1:]
        obs = obs_rows.shape[1]
        size = group_size(windows, parts, members)
        groups = windows // size
        dma = pltpu.SemaphoreType.DMA
        vmem = pl.BlockSpec(memory_space=pltpu.VMEM)
        return pl.pallas_call(
            functools.partial(kernel, groups, size, parts),
            out_shape=pltpu.VMEM(anomalies.shape, F32),
            in_specs=[pl.BlockSpec(memory_space=pltpu.HBM)] * 4,
            out_specs=vmem,
            scratch_shapes=[
                pltpu.VMEM((rows, members), F32),
                pltpu.VMEM((1, rows), F32),
                pltpu.VMEM((1, obs), jnp.int32),
                pltpu.VMEM((1, obs), F32),
                dma((4,)),
                pltpu.VMEM((parts, obs, members), F32),
                pltpu.VMEM((size, parts, members // (2 * parts) + 8, members), F32),
                pltpu.VMEM((size, members, members), F32),
                pltpu.VMEM((size, members, members), BF16),
                pltpu.VMEM((size, members, members), BF16),
                pltpu.VMEM((parts, size, members // (2 * parts) + 8, members), F32),
                pltpu.VMEM((groups, parts, members // parts, members), F32),
                pltpu.VMEM((rows, members), F32),
                dma((parts,)), dma((parts,)),
                dma((size,)), dma((size, parts)),
                dma((size, parts)), dma((size,)),
                dma((groups, parts)), dma((groups,)), dma((parts,)), dma((1,)),
                dma((groups, size)), dma((groups, size)),
                dma((groups, parts)), dma((groups, parts)),
            ],
            compiler_params=pltpu.CompilerParams(
                collective_id=0, has_side_effects=True, vmem_limit_bytes=56 * 1024 * 1024
            ),
        )(anomalies, mean_state, obs_rows, obs_precision)

    placed = (P("win", "state", None), P("win", "state"), P("win", "state"), P("win", "state"))
    return jax.shard_map(
        shards, mesh=mesh, in_specs=placed, out_specs=P("win", "state", None), check_vma=False
    )
```
